128 devices in a mesh: dp: 16 (over z, y), ctx: 8 (over x, core).
Axes of the slice: x: 4, y: 4, z: 4, core: 2. Of those that a mesh axis runs over, the one named last changes fastest.
Arguments:
- history: bfloat16 [16384, 1024], P(('dp', 'ctx')), may hold values from -6 to 6
- grad_output: bfloat16 [16384, 1024], P(('dp', 'ctx')), may hold values from -6 to 6
- lengths: int32 [16, 4], P('dp'), may hold values from 0 to 1024, as said below
- send_order: int32 [16384], P(('dp', 'ctx')), may hold values from 0 to 127, as said below
- place_order: int32 [16384], P(('dp', 'ctx')), may hold values from 0 to 127, as said below
- w_project: bfloat16 [1024, 4096], replicated, may hold values from -0.1875 to 0.1875
- w_out: bfloat16 [1024, 1024], replicated, may hold values from -0.1875 to 0.1875
Outputs:
- output: bfloat16 [16384, 1024], P(('dp', 'ctx'))
- input_grad: bfloat16 [16384, 1024], P(('dp', 'ctx'))
- project_grad: float32 [1024, 4096], P(('dp', 'ctx'))
- mixing_grad: float32 [1024, 1024], P(('dp', 'ctx'))
The draws below stay inside these ranges and needn't reach their ends.
Inputs may be any that keep to these rules, and one draw needn't show every extreme that they name: For each group, the lengths padded up to multiples of 128 sum to 1024; a zero entry occupies no rows. `send_order`: each device's 128 entries name each of its rows once; entries p * 8 to (p + 1) * 8 - 1 are sent to dp index p. `place_order`: each device's 128 entries are a permutation of 0 to 127.
All inputs are finite; a program needn't handle non-finite values.
Results may differ from the reference program's by a relative error of at most 0.014.
Values may be sent and summed in bfloat16 or wider, within the bound.
No kernel may reach another device: no remote copies, remote signals or barrier semaphores. Data moves between devices by JAX's collectives and lax.ppermute only.
A program may use at most 128 MiB of HBM per device.

```python
import jax
import jax.numpy as jnp
from jax import lax

D = 1024
HEADS = 16
R = 128
SEQS = 4
GROUP_ROWS = 1024
ROWS = 16384
N_DP = 16
N_CTX = 8


def draw_lengths(key, part):
    key = jax.random.fold_in(key, 5)
    first_key, second_key, third_key = jax.random.split(key, 3)
    block_count = GROUP_ROWS // 128
    cuts = jnp.sort(jax.random.randint(first_key, (N_DP, SEQS - 1), 0, block_count + 1), axis=1)
    bounds = jnp.concatenate([jnp.zeros((N_DP, 1), jnp.int32), cuts.astype(jnp.int32), jnp.full((N_DP, 1), block_count, jnp.int32)], axis=1)
    counts = bounds[:, 1:] - bounds[:, :-1]
    padding = jax.random.randint(second_key, (N_DP, SEQS), 0, 128)
    drawn = jnp.where(counts > 0, counts * 128 - padding, 0)
    chosen = jax.random.randint(third_key, (), 0, N_DP)
    forced = jnp.where(jnp.arange(SEQS) == 0, block_count * 128, 0)[None, :]
    result = jnp.where((jnp.arange(N_DP) == chosen)[:, None], forced, drawn)
    return result.astype(jnp.int32)


def draw_send_order(key, part):
    key = jax.random.fold_in(key, 11)
    device_keys = jax.random.split(key, ROWS // R)
    orders = jax.vmap(lambda single: jax.random.permutation(single, R))(device_keys)
    return orders.reshape(-1).astype(jnp.int32)


def draw_place_order(key, part):
    key = jax.random.fold_in(key, 17)
    device_keys = jax.random.split(key, ROWS // R)
    orders = jax.vmap(lambda single: jax.random.permutation(single, R))(device_keys)
    return orders.reshape(-1).astype(jnp.int32)


def levels(own_key, shape, pieces, low, largest):
    def one(dim, shards_of):
        steps = jax.random.uniform(jax.random.fold_in(jax.random.fold_in(own_key, 6), dim), (shards_of,), jnp.float32, low / len(pieces), largest / len(pieces))
        return jnp.repeat(jnp.exp(steps), shape[dim] // shards_of).reshape((-1,) + (1,) * (len(shape) - dim - 1))

    loudness = one(*pieces[0])
    for cut in pieces[1:]:
        loudness = loudness * one(*cut)
    return loudness


def normal_values(rng, extent, scale, most, shards=(), kind=jnp.bfloat16):
    values = jax.random.normal(rng, extent, jnp.float32) * scale
    if len(shards) > 0:
        values = levels(rng, extent, shards, -0.22, 0.18) * values
    return jnp.clip(values, min=-most, max=most).astype(kind)


def setup_inputs(seed: int = 0) -> dict:
    seeds = jax.random.split(jax.random.key(seed), 8)
    return {
        "history": normal_values(seeds[0], (ROWS, D), 1.0, 6.0, ((0, 128),)),
        "grad_output": normal_values(seeds[1], (ROWS, D), 1.0, 6.0, ((0, 128),)),
        "lengths": draw_lengths(jax.random.fold_in(seeds[7], 71), 0),
        "send_order": draw_send_order(jax.random.fold_in(seeds[7], 71), 0),
        "place_order": draw_place_order(jax.random.fold_in(seeds[7], 71), 0),
        "w_project": normal_values(seeds[5], (D, 4 * D), D ** -0.5, 0.1875),
        "w_out": normal_values(seeds[6], (D, D), D ** -0.5, 0.1875),
    }


epsilon = 1e-06
padding_unit = 128

def silu_slope(values):
    sigma = jax.nn.sigmoid(values)
    return sigma * (1.0 + values * (1.0 - sigma))

def layer_norm(values):
    middle = lax.optimization_barrier(jnp.mean(values, axis=-1, keepdims=True))
    centred = values - middle
    inverse = lax.rsqrt(lax.optimization_barrier(jnp.mean(centred * centred, axis=-1, keepdims=True)) + epsilon)
    return (centred * inverse, inverse)

def norm_back(gradient, normed, inverse):
    first = lax.optimization_barrier(jnp.mean(gradient, axis=-1, keepdims=True))
    second = lax.optimization_barrier(jnp.mean(gradient * normed, axis=-1, keepdims=True))
    return inverse * (gradient - first - normed * second)

def row_layout(group_lengths, row_ids):
    blocks = (group_lengths + (padding_unit - 1)) // padding_unit
    ends = jnp.cumsum(blocks * padding_unit)
    starts = ends - blocks * padding_unit
    segment = lax.optimization_barrier(jnp.sum((ends[None, :] <= row_ids[:, None]).astype(jnp.int32), axis=1))
    onehot = (segment[:, None] == jnp.arange(group_lengths.shape[0], dtype=jnp.int32)[None, :]).astype(jnp.int32)
    position = row_ids - lax.optimization_barrier(jnp.sum(onehot * starts[None, :], axis=1))
    live = position < lax.optimization_barrier(jnp.sum(onehot * group_lengths[None, :], axis=1))
    return (segment, position, live)

def attend_rows(query_rows, key_rows, value_rows, visible, score_scale):
    scores = jnp.einsum('rhd,lhd->hrl', query_rows.astype(jnp.float32), key_rows.astype(jnp.float32)) * score_scale
    weights = jnp.where(visible[None], jax.nn.silu(scores), 0.0).astype(jnp.bfloat16)
    return jnp.einsum('hrl,lhd->rhd', weights.astype(jnp.float32), value_rows.astype(jnp.float32))

def attend_back(query_rows, key_rows, value_rows, visible, score_scale, grad_att):
    scores = jnp.einsum('rhd,lhd->hrl', query_rows.astype(jnp.float32), key_rows.astype(jnp.float32)) * score_scale
    weights = jnp.where(visible[None], jax.nn.silu(scores), 0.0).astype(jnp.bfloat16)
    grad_weights = jnp.einsum('rhd,lhd->hrl', grad_att.astype(jnp.float32), value_rows.astype(jnp.float32))
    grad_scores = (jnp.where(visible[None], grad_weights * silu_slope(scores), 0.0) * score_scale).astype(jnp.bfloat16)
    grad_query = jnp.einsum('hrl,lhd->rhd', grad_scores.astype(jnp.float32), key_rows.astype(jnp.float32))
    grad_key = jnp.einsum('hrl,rhd->lhd', grad_scores.astype(jnp.float32), query_rows.astype(jnp.float32))
    grad_value = jnp.einsum('hrl,rhd->lhd', weights.astype(jnp.float32), grad_att.astype(jnp.float32))
    return (grad_query, grad_key, grad_value)

def reference(history, grad_output, lengths, send_order, place_order, w_project, w_out):
    quota = R // N_DP
    group_rows = N_CTX * R
    head_width = D // HEADS
    score_scale = head_width ** (-0.5)
    sender = send_order.reshape(N_DP, N_CTX, R)
    placer = place_order.reshape(N_DP, N_CTX, R)
    group_ids = jnp.arange(N_DP, dtype=jnp.int32)[:, None, None]
    ctx_ids = jnp.arange(N_CTX, dtype=jnp.int32)[None, :, None]
    source_peer = placer // quota
    source_slot = placer % quota
    source_local = sender[source_peer, ctx_ids, group_ids * quota + source_slot]
    anchor = ((source_peer * N_CTX + ctx_ids) * R + source_local).reshape(N_DP, group_rows).astype(jnp.int32)
    row_ids = jnp.arange(group_rows, dtype=jnp.int32)

    def group_pass(carried, item):
        anchor_rows, group_lengths = item
        inputs = history[anchor_rows]
        upstream = grad_output[anchor_rows]
        segment, position, live = row_layout(group_lengths, row_ids)
        visible = (segment[:, None] == segment[None, :]) & (position[None, :] <= position[:, None]) & live[:, None]
        normed, inverse = layer_norm(inputs.astype(jnp.float32))
        normed_bf = normed.astype(jnp.bfloat16)
        pre = jnp.dot(normed_bf, w_project, preferred_element_type=jnp.float32)
        proj = jax.nn.silu(pre).astype(jnp.bfloat16)
        gate_rows = proj[:, :D]
        value_rows = proj[:, D:2 * D].reshape(group_rows, HEADS, head_width)
        query_rows = proj[:, 2 * D:3 * D].reshape(group_rows, HEADS, head_width)
        key_rows = proj[:, 3 * D:].reshape(group_rows, HEADS, head_width)
        query_blocks = query_rows.reshape(N_CTX, R, HEADS, head_width)
        visible_blocks = visible.reshape(N_CTX, R, group_rows)
        attended = lax.map(lambda pair: attend_rows(pair[0], key_rows, value_rows, pair[1], score_scale), (query_blocks, visible_blocks))
        attended = attended.reshape(group_rows, D)
        zvalue, zinverse = layer_norm(attended)
        hidden = (zvalue * gate_rows.astype(jnp.float32)).astype(jnp.bfloat16)
        packed_out = (jnp.dot(hidden, w_out, preferred_element_type=jnp.float32) + inputs.astype(jnp.float32)).astype(jnp.bfloat16)
        grad_hidden = jnp.dot(upstream, w_out.T, preferred_element_type=jnp.float32)
        mixing_part = jnp.dot(hidden.T, upstream, preferred_element_type=jnp.float32)
        grad_z = grad_hidden * gate_rows.astype(jnp.float32)
        grad_gate = grad_hidden * zvalue
        grad_att = norm_back(grad_z, zvalue, zinverse).astype(jnp.bfloat16)
        grad_blocks = grad_att.reshape(N_CTX, R, HEADS, head_width)

        def block_back(triple):
            grad_query, grad_key, grad_value = attend_back(triple[0], key_rows, value_rows, triple[1], score_scale, triple[2])
            return (grad_query, grad_key.astype(jnp.bfloat16), grad_value.astype(jnp.bfloat16))
        grad_query, key_parts, value_parts = lax.map(block_back, (query_blocks, visible_blocks, grad_blocks))
        grad_key = lax.optimization_barrier(jnp.sum(key_parts.astype(jnp.float32), axis=0)).reshape(group_rows, D)
        grad_value = lax.optimization_barrier(jnp.sum(value_parts.astype(jnp.float32), axis=0)).reshape(group_rows, D)
        grad_query = grad_query.reshape(group_rows, D)
        grad_pre = (jnp.concatenate([grad_gate, grad_value, grad_query, grad_key], axis=1) * silu_slope(pre)).astype(jnp.bfloat16)
        project_part = jnp.dot(normed_bf.T, grad_pre, preferred_element_type=jnp.float32)
        grad_normed = jnp.dot(grad_pre, w_project.T, preferred_element_type=jnp.float32)
        packed_grad = (norm_back(grad_normed, normed, inverse) + upstream.astype(jnp.float32)).astype(jnp.bfloat16)
        return ((carried[0] + project_part, carried[1] + mixing_part), (packed_out, packed_grad))
    start = (jnp.zeros((D, 4 * D), jnp.float32), jnp.zeros((D, D), jnp.float32))
    sums, packed = lax.scan(group_pass, start, (anchor, lengths))
    flat_anchor = anchor.reshape(-1)
    output = jnp.zeros((N_DP * group_rows, D), jnp.bfloat16).at[flat_anchor].set(packed[0].reshape(-1, D))
    input_grad = jnp.zeros((N_DP * group_rows, D), jnp.bfloat16).at[flat_anchor].set(packed[1].reshape(-1, D))
    return (output, input_grad, sums[0], sums[1])
```

```python
import jax
import jax.numpy as jnp
from jax import lax
from jax.experimental import pallas as pl
from jax.experimental.pallas import tpu as pltpu
from jax.sharding import PartitionSpec as P


D = 1024
WIDE = 128
HEAD = 64
N_DP = 16
N_CTX = 8
R = 128
GROUP = 1024
BLOCK = 256
EPS = 1e-6
BF = jnp.bfloat16
F32 = jnp.float32
NN = (((1,), (0,)), ((), ()))
NT = (((1,), (1,)), ((), ()))


def dot(a, b, dims=NN):
    return lax.dot_general(a, b, dims, preferred_element_type=F32)


def sigmoid(v):
    return 0.5 * jnp.tanh(0.5 * v) + 0.5


def iota(shape, dim):
    return lax.broadcasted_iota(jnp.int32, shape, dim)


def row_norm(values):
    centred = values - jnp.mean(values, axis=-1, keepdims=True)
    inverse = lax.rsqrt(jnp.mean(centred * centred, axis=-1, keepdims=True) + EPS)
    return centred * inverse, inverse


def call(body, outs, *args, smem=0, scratch=()):
    specs = [pl.BlockSpec(memory_space=pltpu.SMEM)] * smem
    specs += [pl.BlockSpec(memory_space=pltpu.VMEM)] * (len(args) - smem)
    return pl.pallas_call(
        body,
        out_shape=[jax.ShapeDtypeStruct(s, t) for s, t in outs],
        in_specs=specs,
        out_specs=[pl.BlockSpec(memory_space=pltpu.VMEM)] * len(outs),
        scratch_shapes=list(scratch),
        compiler_params=pltpu.CompilerParams(vmem_limit_bytes=48 * 1024 * 1024),
    )(*args)


REL = [(0, 0), (0, 1), (1, 0), (1, 1), (2, 0), (2, 1), (3, 0), (3, 1)]


def place_of(ctx, rel):
    chip = lax.rem((ctx >> 1) + rel[0], 4)
    return chip * 2 + ((ctx & 1) ^ rel[1])


def send(x, step, flip):
    pairs = [(2 * a + b, 2 * ((a + step) % 4) + (b ^ flip)) for a in range(4) for b in range(2)]
    return lax.ppermute(x, "ctx", pairs)


def ring_gather(x):
    half = x.shape[0] // 2
    up = send(x, 3, 0)
    down = send(x, 1, 0)
    far = (send(up[:half], 3, 0), send(down[half:], 1, 0))
    return [
        x,
        send(x, 0, 1),
        up,
        send(up, 0, 1),
        far[0],
        far[1],
        send(far[0], 0, 1),
        send(far[1], 0, 1),
        down,
        send(down, 0, 1),
    ]


def join(refs):
    far = [jnp.concatenate([refs[i][...], refs[i + 1][...]], axis=0) for i in (4, 6)]
    return [refs[0][...], refs[1][...], refs[2][...], refs[3][...], *far, refs[8][...], refs[9][...]]


def exchange(parts):
    got = {(0, 0): parts[0]}
    for part, (step, flip) in zip(parts[1:], REL[1:]):
        got[((4 - step) % 4, flip)] = send(part, step, flip)
    return [got[rel] for rel in REL]


def at(index):
    return pl.ds(pl.multiple_of(index * R, R), R)


def pack_kernel(hist, gout, order, out):
    xn = row_norm(hist[...].astype(F32))[0].astype(BF)
    pick = (order[...] == iota((R, R), 1)).astype(BF)
    a = dot(pick, xn).reshape(N_DP, 8, D)
    b = dot(pick, gout[...]).reshape(N_DP, 8, D)
    out[...] = jnp.concatenate([a, b], axis=1).reshape(2 * R, D).astype(BF)


def place_kernel(recv, place, xt, up):
    at_row = (place[...] >> 3) * 16 + (place[...] & 7)
    lanes = iota((R, 2 * R), 1)
    x = dot((at_row == lanes).astype(BF), recv[...])
    xt[...] = x.T.astype(BF)
    up[...] = dot((at_row + 8 == lanes).astype(BF), recv[...]).astype(BF)


def first_visible(lengths):
    rows = iota((1, GROUP), 1)
    low = jnp.full((1, GROUP), 1 << 20, jnp.int32)
    start = jnp.int32(0)
    for j in range(4):
        length = lengths[0, j]
        low = jnp.where((rows >= start) & (rows < start + length), start, low)
        start = start + ((length + 127) >> 7) * 128
    return low


def visible_block(low, rb, tb):
    rs = slice(rb * BLOCK, (rb + 1) * BLOCK)
    keys = iota((BLOCK, BLOCK), 0) + tb * BLOCK
    seen = keys >= low[:, rs]
    if tb == rb:
        seen = seen & (keys <= iota((BLOCK, BLOCK), 1) + rb * BLOCK)
    return seen


def masked_head(x, h, scale=None):
    rows = iota(x.shape, 0)
    x = jnp.where((rows >= h * HEAD) & (rows < (h + 1) * HEAD), x, 0.0)
    if scale is not None:
        x = x * scale
    return x.astype(BF)


def forward_kernel(lengths, ctx, wt, *refs):
    shards = refs[:10]
    xn, pre, proj, att = refs[10:]
    c = ctx[0]
    for value, rel in zip(join(shards), REL):
        xn[:, at(place_of(c, rel))] = value
    for n in range(GROUP // BLOCK):
        cols = slice(n * BLOCK, (n + 1) * BLOCK)
        p = dot(wt[...], xn[:, cols])
        pre[:, cols] = p
        proj[:, cols] = (p * sigmoid(p)).astype(BF)
    low = first_visible(lengths)
    keys = proj[3 * WIDE :, :].astype(F32).T.astype(BF)
    for rb in range(GROUP // BLOCK):
        rs = slice(rb * BLOCK, (rb + 1) * BLOCK)
        query = proj[2 * WIDE : 3 * WIDE, rs].astype(F32)
        for h in range(2):
            hs = slice(h * HEAD, (h + 1) * HEAD)
            vs = slice(WIDE + h * HEAD, WIDE + (h + 1) * HEAD)
            q = masked_head(query, h, 0.125)
            total = jnp.zeros((HEAD, BLOCK), F32)
            for tb in range(rb + 1):
                ts = slice(tb * BLOCK, (tb + 1) * BLOCK)
                s = dot(keys[ts], q)
                w = jnp.where(visible_block(low, rb, tb), s * sigmoid(s), 0.0).astype(BF)
                total = total + dot(proj[vs, ts], w)
            att[hs, rs] = total


def sums_kernel(ctx, w, proj, att, *refs):
    shards = refs[:10]
    gh, sums = refs[10:]
    c = ctx[0]
    for value, rel in zip(join(shards), REL):
        gh[:, at(place_of(c, rel))] = dot(w[...], value, NT)
    a = att[...]
    mean = jnp.mean(a, axis=0, keepdims=True)
    dev = a - mean
    gz = gh[...] * proj[:WIDE, :].astype(F32)
    sums[0:1, :] = mean
    sums[1:2, :] = jnp.sum(dev * dev, axis=0, keepdims=True)
    sums[2:3, :] = jnp.sum(gz, axis=0, keepdims=True)
    sums[3:4, :] = jnp.sum(gz * dev, axis=0, keepdims=True)
    sums[4:8, :] = jnp.zeros((4, GROUP), F32)


def norm_kernel(ctx, proj, att, gh, pre, *refs):
    sums, shards = refs[:8], refs[8:18]
    hidden, (gatt, ggate, mixing) = refs[18:26], refs[26:29]
    c = ctx[0]
    each = [s[...] for s in sums]
    mean = sum(s[0:1, :] for s in each) * (1.0 / N_CTX)
    spread = sum(s[1:2, :] + WIDE * jnp.square(s[0:1, :] - mean) for s in each)
    inverse = lax.rsqrt(spread * (1.0 / D) + EPS)
    first = sum(s[2:3, :] for s in each) * (1.0 / D)
    second = sum(s[3:4, :] + (s[0:1, :] - mean) * s[2:3, :] for s in each) * inverse * (1.0 / D)
    z = (att[...] - mean) * inverse
    gate = proj[:WIDE, :].astype(F32)
    hid = (z * gate).astype(BF)
    gatt[...] = (inverse * (gh[...] * gate - first - z * second)).astype(BF)
    p = pre[:WIDE, :]
    sig = sigmoid(p)
    ggate[...] = (gh[...] * z * (sig * (1.0 + p * (1.0 - sig)))).astype(BF)
    att_hidden = refs[29]
    att_hidden[...] = hid
    total = jnp.zeros((WIDE, D), F32)
    for i, (value, rel) in enumerate(zip(join(shards), REL)):
        piece = att_hidden[:, at(place_of(c, rel))]
        hidden[i][...] = piece
        total = total + dot(piece, value)
    mixing[...] = total.astype(BF)


def backward_kernel(lengths, ctx, pre, proj, gatt, ggate, *refs):
    parts, gp, (dk, dv) = refs[:8], refs[8], refs[9:11]
    c = ctx[0]
    low = first_visible(lengths)
    keys = proj[3 * WIDE :, :].astype(F32).T.astype(BF)
    values = proj[WIDE : 2 * WIDE, :].astype(F32).T.astype(BF)
    dk[...] = jnp.zeros((WIDE, GROUP), F32)
    dv[...] = jnp.zeros((WIDE, GROUP), F32)

    def slope(v):
        sig = sigmoid(v)
        return sig * (1.0 + v * (1.0 - sig))

    gp[:WIDE, :] = ggate[...]
    for rb in range(GROUP // BLOCK):
        rs = slice(rb * BLOCK, (rb + 1) * BLOCK)
        query = proj[2 * WIDE : 3 * WIDE, rs].astype(F32)
        grad = gatt[:, rs].astype(F32)
        for h in range(2):
            hs = slice(h * HEAD, (h + 1) * HEAD)
            q = masked_head(query, h, 0.125)
            g = masked_head(grad, h)
            total = jnp.zeros((HEAD, BLOCK), F32)
            for tb in range(rb + 1):
                ts = slice(tb * BLOCK, (tb + 1) * BLOCK)
                s = dot(keys[ts], q)
                gw = dot(values[ts], g)
                seen = visible_block(low, rb, tb)
                sig = sigmoid(s)
                w = jnp.where(seen, s * sig, 0.0)
                gs = jnp.where(seen, gw * (sig + w * (1.0 - sig)), 0.0).astype(BF)
                dv[hs, ts] += dot(g[hs], w.astype(BF), NT)
                dk[hs, ts] += dot(q[hs], gs, NT)
                total = total + dot(proj[3 * WIDE + h * HEAD : 3 * WIDE + (h + 1) * HEAD, ts], gs)
            qs = slice(2 * WIDE + h * HEAD, 2 * WIDE + (h + 1) * HEAD)
            gp[qs, rs] = (total * 0.125 * slope(pre[qs, rs])).astype(BF)
    gp[WIDE : 2 * WIDE, :] = (dv[...] * slope(pre[WIDE : 2 * WIDE, :])).astype(BF)
    gp[3 * WIDE :, :] = (dk[...] * slope(pre[3 * WIDE :, :])).astype(BF)
    for part, rel in zip(parts, REL):
        part[...] = gp[:, at(place_of(c, rel))]


def project_kernel(xn, gp, out):
    for n in range(4):
        rows = slice(n * BLOCK, (n + 1) * BLOCK)
        out[rows, :] = dot(xn[rows, :], gp[...], NT).astype(BF)


def finish_kernel(ctx, place, w_project, w_out, mixing, *refs):
    hidden, grads, out, (hid, gp) = refs[:8], refs[8:16], refs[16], refs[17:19]
    c = ctx[0]
    for value, grad, rel in zip(hidden, grads, REL):
        src = place_of(c, rel)
        hid[at(src), :] = value[...]
        for kind in range(4):
            gp[at(kind * 8 + src), :] = grad[kind * WIDE : (kind + 1) * WIDE, :]
    back = (place[...] == iota((R, R), 0)).astype(BF)
    o = dot(dot(back, hid[...], NT).astype(BF), w_out[...])
    gx = dot(w_project[...], gp[...])
    gx = dot(back, gx.astype(BF), NT)
    mix = mixing[...].astype(F32)
    parts = [v.reshape(N_DP, 8, D) for v in (o, gx, mix)]
    out[...] = jnp.concatenate(parts, axis=1).reshape(3 * R, D).astype(BF)


def unpack_kernel(recv, hist, gout, order, out, grad, mixing):
    got = recv[...].astype(F32).reshape(N_DP, 24, D)
    back = (order[...] == iota((R, R), 0)).astype(BF)
    o = dot(back, got[:, 0:8].reshape(R, D).astype(BF))
    gx = dot(back, got[:, 8:16].reshape(R, D).astype(BF))
    x = hist[...].astype(F32)
    out[...] = (o + x).astype(BF)
    normed, inverse = row_norm(x)
    first = jnp.mean(gx, axis=-1, keepdims=True)
    second = jnp.mean(gx * normed, axis=-1, keepdims=True)
    grad[...] = (inverse * (gx - first - normed * second) + gout[...].astype(F32)).astype(BF)
    mixing[...] = jnp.sum(got[:, 16:24], axis=0)


def weight_kernel(recv, out):
    total = jnp.sum(recv[...].astype(F32).reshape(N_DP, N_CTX, 8, 4 * WIDE), axis=0)
    for c in range(N_CTX):
        for kind in range(4):
            start = kind * D + c * WIDE
            out[:, start : start + WIDE] = total[c, :, kind * WIDE : (kind + 1) * WIDE]


def local(history, grad_output, lengths, send_order, place_order, w_project, w_out):
    ctx = lax.axis_index("ctx").astype(jnp.int32)
    ctx_s = ctx.reshape(1)
    first = ctx * WIDE
    w_own = jnp.concatenate(
        [lax.dynamic_slice_in_dim(w_project, kind * D + first, WIDE, 1) for kind in range(4)], axis=1
    ).T
    w_out_own = lax.dynamic_slice_in_dim(w_out, first, WIDE, 0)

    (packed,) = call(
        pack_kernel, [((2 * R, D), BF)], history, grad_output, send_order.reshape(R, 1)
    )
    arrived = lax.all_to_all(packed, "dp", split_axis=0, concat_axis=0, tiled=True)
    xt, up = call(
        place_kernel, [((D, R), BF), ((R, D), BF)], arrived, place_order.reshape(R, 1)
    )
    xt_shards = ring_gather(xt)
    up_shards = ring_gather(up)

    xn, pre, proj, att = call(
        forward_kernel,
        [((D, GROUP), BF), ((4 * WIDE, GROUP), F32), ((4 * WIDE, GROUP), BF), ((WIDE, GROUP), F32)],
        lengths,
        ctx_s,
        w_own,
        *xt_shards,
        smem=2,
    )
    gh, sums = call(
        sums_kernel,
        [((WIDE, GROUP), F32), ((8, GROUP), F32)],
        ctx_s,
        w_out_own,
        proj,
        att,
        *up_shards,
        smem=1,
    )
    all_sums = [sums] + [send(sums, step, flip) for step, flip in REL[1:]]
    *hidden, gatt, ggate, mixing = call(
        norm_kernel,
        [((WIDE, R), BF)] * 8 + [((WIDE, GROUP), BF)] * 2 + [((WIDE, D), BF)],
        ctx_s,
        proj,
        att,
        gh,
        pre,
        *all_sums,
        *up_shards,
        smem=1,
        scratch=[pltpu.VMEM((WIDE, GROUP), BF)],
    )
    hidden = exchange(hidden)
    *grads, gp = call(
        backward_kernel,
        [((4 * WIDE, R), BF)] * 8 + [((4 * WIDE, GROUP), BF)],
        lengths,
        ctx_s,
        pre,
        proj,
        gatt,
        ggate,
        smem=2,
        scratch=[pltpu.VMEM((WIDE, GROUP), F32)] * 2,
    )
    grads = exchange(grads)
    (project,) = call(project_kernel, [((D, 4 * WIDE), BF)], xn, gp)
    project = lax.all_to_all(project, ("dp", "ctx"), split_axis=0, concat_axis=0, tiled=True)

    (returned,) = call(
        finish_kernel,
        [((3 * R, D), BF)],
        ctx_s,
        place_order.reshape(1, R),
        w_project,
        w_out,
        mixing,
        *hidden,
        *grads,
        smem=1,
        scratch=[pltpu.VMEM((D, R), BF), pltpu.VMEM((4 * D, R), BF)],
    )
    returned = lax.all_to_all(returned, "dp", split_axis=0, concat_axis=0, tiled=True)
    output, input_grad, mixing_part = call(
        unpack_kernel,
        [((R, D), BF), ((R, D), BF), ((8, D), F32)],
        returned,
        history,
        grad_output,
        send_order.reshape(1, R),
    )
    (project_grad,) = call(weight_kernel, [((8, 4 * D), F32)], project)
    owners = [(d * 8 + c, (2 * c + d // 8) * 8 + d % 8) for d in range(N_DP) for c in range(N_CTX)]
    mixing_grad = lax.ppermute(mixing_part, ("dp", "ctx"), owners)
    return output, input_grad, project_grad, mixing_grad


def solution(mesh):
    rows = P(("dp", "ctx"), None)
    ids = P(("dp", "ctx"))
    return jax.shard_map(
        local,
        mesh=mesh,
        in_specs=(rows, rows, P("dp", None), ids, ids, P(), P()),
        out_specs=(rows, rows, rows, rows),
        check_vma=False,
    )
```

```python
import jax
import jax.numpy as jnp
from jax import lax
from jax.experimental import pallas as pl
from jax.experimental.pallas import tpu as pltpu
from jax.sharding import PartitionSpec as P


D = 1024
WIDE = 128
PART = 5 * WIDE
HEAD = 64
N_DP = 16
N_CTX = 8
R = 128
GROUP = 1024
BLOCK = 256
EPS = 1e-6
BF = jnp.bfloat16
F32 = jnp.float32
NN = (((1,), (0,)), ((), ()))
NT = (((1,), (1,)), ((), ()))
VMEM_BYTES = 32 * 1024 * 1024


def dot(a, b, dims=NN):
    return lax.dot_general(a, b, dims, preferred_element_type=F32)


def sigmoid(v):
    return 0.5 * jnp.tanh(0.5 * v) + 0.5


def iota(shape, dim):
    return lax.broadcasted_iota(jnp.int32, shape, dim)


def row_norm(values):
    centred = values - jnp.mean(values, axis=-1, keepdims=True)
    inverse = lax.rsqrt(jnp.mean(centred * centred, axis=-1, keepdims=True) + EPS)
    return centred * inverse, inverse


def skip(body, first, count):
    def kernel(*refs):
        body(*refs[:first], *refs[first + count :])

    return kernel if count else body


def hbm(x):
    return pltpu.with_memory_space_constraint(x, pltpu.HBM)


def call(body, outs, *args, smem=0, plain=0, scratch=(), late=()):
    specs = [pl.BlockSpec(memory_space=pltpu.SMEM)] * smem
    specs += [pl.BlockSpec(memory_space=pltpu.VMEM)] * (len(args) - smem - plain)
    specs += [pl.BlockSpec(memory_space=pl.ANY)] * (plain + len(late))
    return pl.pallas_call(
        skip(body, len(args), len(late)),
        out_shape=[pltpu.HBM(s, t) for s, t in outs],
        in_specs=specs,
        out_specs=[pl.BlockSpec(memory_space=pltpu.VMEM)] * len(outs),
        scratch_shapes=list(scratch),
        compiler_params=pltpu.CompilerParams(vmem_limit_bytes=VMEM_BYTES),
    )(*args, *late)


REL = [(0, 0), (0, 1), (1, 0), (1, 1), (2, 0), (2, 1), (3, 0), (3, 1)]


def place_of(ctx, rel):
    chip = lax.rem((ctx >> 1) + rel[0], 4)
    return chip * 2 + ((ctx & 1) ^ rel[1])


def send(x, step, flip):
    pairs = [(2 * a + b, 2 * ((a + step) % 4) + (b ^ flip)) for a in range(4) for b in range(2)]
    return lax.ppermute(x, "ctx", pairs)


def ring_gather(x):
    half = x.shape[0] // 2
    up = send(x, 3, 0)
    down = send(x, 1, 0)
    far = (send(up[:half], 3, 0), send(down[half:], 1, 0))
    shards = [x, send(x, 0, 1), up, send(up, 0, 1), *far]
    shards += [send(far[0], 0, 1), send(far[1], 0, 1), down, send(down, 0, 1)]
    return shards


def relay(own, other, near, far):
    far = [send(send(far[0], 1, 0), 1, 0), send(send(far[1], 3, 0), 3, 0)]
    near = [send(near[0], 1, 0), send(near[1], 3, 0)]
    got = [own, send(other, 0, 1)]
    for v in near + far:
        got += [v, send(v, 0, 1)]
    return got


def at(index):
    return pl.ds(pl.multiple_of(index * R, R), R)


def copy_kernel(ctx, x, out):
    del ctx
    out[...] = x[...]


def pick_rows(ids):
    return (ids == iota((R, R), 0)).astype(F32).T.astype(BF)


def pack_kernel(hist, gout, order, out):
    xn = row_norm(hist[...].astype(F32))[0].astype(BF)
    pick = pick_rows(order[...])
    a = dot(pick, xn).reshape(N_DP, 8, D)
    b = dot(pick, gout[...]).reshape(N_DP, 8, D)
    out[...] = jnp.concatenate([a, b], axis=1).reshape(2 * R, D).astype(BF)


def own_weights_kernel(ctx, w, out):
    del ctx
    out[...] = w[...].astype(F32).T.astype(BF)


def place_kernel(recv, place, out):
    pick = pick_rows(place[...])
    got = recv[...].astype(F32).reshape(N_DP, 2, 8, D)
    for i in range(2):
        rows = dot(pick, got[:, i].reshape(R, D).astype(BF))
        out[i * D : (i + 1) * D, :] = rows.T.astype(BF)


def first_visible(lengths):
    rows = iota((1, GROUP), 1)
    low = jnp.full((1, GROUP), 1 << 20, jnp.int32)
    start = jnp.int32(0)
    for j in range(4):
        length = lengths[0, j]
        low = jnp.where((rows >= start) & (rows < start + length), start, low)
        start = start + ((length + 127) >> 7) * 128
    return low


def visible_block(low, rb, tb):
    rs = slice(rb * BLOCK, (rb + 1) * BLOCK)
    keys = iota((BLOCK, BLOCK), 0) + tb * BLOCK
    seen = keys >= low[:, rs]
    if tb == rb:
        seen = seen & (keys <= iota((BLOCK, BLOCK), 1) + rb * BLOCK)
    return seen


def masked_head(x, h, scale=None):
    rows = iota(x.shape, 0)
    x = jnp.where((rows >= h * HEAD) & (rows < (h + 1) * HEAD), x, 0.0)
    if scale is not None:
        x = x * scale
    return x.astype(BF)


def forward_kernel(lengths, ctx, wt, w_out, *refs):
    shards = refs[:10]
    xn, up, slopes, proj, att, gh, sums = refs[10:]
    c = ctx[0]
    for i, rel in zip((0, 1, 2, 3, 8, 9), REL[:4] + REL[6:]):
        to = at(place_of(c, rel))
        xn[:, to] = shards[i][:D, :]
        up[:, to] = shards[i][D:, :]
    for i, core in ((4, 0), (6, 1)):
        to = at(place_of(c, (2, core)))
        xn[:, to] = shards[i][...]
        up[:, to] = shards[i + 1][...]
    for n in range(GROUP // BLOCK):
        cols = slice(n * BLOCK, (n + 1) * BLOCK)
        p = dot(wt[...], xn[:, cols])
        sig = sigmoid(p)
        out = p * sig
        slopes[:, cols] = (sig + out * (1.0 - sig)).astype(BF)
        proj[:, cols] = out.astype(BF)
        gh[:, cols] = dot(w_out[...], up[:, cols])
    low = first_visible(lengths)
    keys = proj[3 * WIDE :, :].astype(F32).T.astype(BF)
    for rb in range(GROUP // BLOCK):
        rs = slice(rb * BLOCK, (rb + 1) * BLOCK)
        query = proj[2 * WIDE : 3 * WIDE, rs].astype(F32)
        for h in range(2):
            hs = slice(h * HEAD, (h + 1) * HEAD)
            q = masked_head(query, h, 0.125)
            total = jnp.zeros((HEAD, BLOCK), F32)
            for tb in range(rb + 1):
                ts = slice(tb * BLOCK, (tb + 1) * BLOCK)
                s = dot(keys[ts], q)
                w = jnp.where(visible_block(low, rb, tb), s * sigmoid(s), 0.0).astype(BF)
                total = total + dot(proj[WIDE + h * HEAD : WIDE + (h + 1) * HEAD, ts], w)
            att[hs, rs] = total
    a = att[...]
    mean = jnp.mean(a, axis=0, keepdims=True)
    dev = a - mean
    gz = gh[...] * proj[:WIDE, :].astype(F32)
    sums[0:1, :] = mean
    sums[1:2, :] = jnp.sum(dev * dev, axis=0, keepdims=True)
    sums[2:3, :] = jnp.sum(gz, axis=0, keepdims=True)
    sums[3:4, :] = jnp.sum(gz * dev, axis=0, keepdims=True)
    sums[4:8, :] = jnp.zeros((4, GROUP), F32)


def backward_kernel(lengths, ctx, slopes, proj, att, gh, *refs):
    sums, (xn_hbm, up_hbm) = refs[:8], refs[8:10]
    own, other, up_part, down_part, far_up, far_down, weights = refs[10:17]
    gp, gatt, dk, dv, xn, up, sems = refs[17:]
    loads = [
        pltpu.make_async_copy(xn_hbm, xn, sems.at[0]),
        pltpu.make_async_copy(up_hbm, up, sems.at[1]),
    ]
    for load in loads:
        load.start()
    c = ctx[0]
    each = [s[...] for s in sums]
    mean = sum(s[0:1, :] for s in each) * (1.0 / N_CTX)
    spread = sum(s[1:2, :] + WIDE * jnp.square(s[0:1, :] - mean) for s in each)
    inverse = lax.rsqrt(spread * (1.0 / D) + EPS)
    first = sum(s[2:3, :] for s in each) * (1.0 / D)
    second = sum(s[3:4, :] + (s[0:1, :] - mean) * s[2:3, :] for s in each) * inverse * (1.0 / D)
    for n in range(GROUP // BLOCK):
        cols = slice(n * BLOCK, (n + 1) * BLOCK)
        z = (att[:, cols] - mean[:, cols]) * inverse[:, cols]
        gate = proj[:WIDE, cols].astype(F32)
        grad = gh[:, cols]
        gp[:WIDE, cols] = (z * gate).astype(BF)
        gp[WIDE : 2 * WIDE, cols] = (grad * z * slopes[:WIDE, cols].astype(F32)).astype(BF)
        rest = grad * gate - first[:, cols] - z * second[:, cols]
        gatt[:, cols] = (inverse[:, cols] * rest).astype(BF)

    low = first_visible(lengths)
    keys = proj[3 * WIDE :, :].astype(F32).T.astype(BF)
    values = proj[WIDE : 2 * WIDE, :].astype(F32).T.astype(BF)
    dk[...] = jnp.zeros((WIDE, GROUP), F32)
    dv[...] = jnp.zeros((WIDE, GROUP), F32)
    for rb in range(GROUP // BLOCK):
        rs = slice(rb * BLOCK, (rb + 1) * BLOCK)
        query = proj[2 * WIDE : 3 * WIDE, rs].astype(F32)
        grad = gatt[:, rs].astype(F32)
        for h in range(2):
            hs = slice(h * HEAD, (h + 1) * HEAD)
            q = masked_head(query, h, 0.125)
            g = masked_head(grad, h)
            total = jnp.zeros((HEAD, BLOCK), F32)
            for tb in range(rb + 1):
                ts = slice(tb * BLOCK, (tb + 1) * BLOCK)
                s = dot(keys[ts], q)
                gw = dot(values[ts], g)
                seen = visible_block(low, rb, tb)
                sig = sigmoid(s)
                w = jnp.where(seen, s * sig, 0.0)
                gs = jnp.where(seen, gw * (sig + w * (1.0 - sig)), 0.0).astype(BF)
                dv[hs, ts] += dot(g[hs], w.astype(BF), NT)
                dk[hs, ts] += dot(q[hs], gs, NT)
                total = total + dot(proj[3 * WIDE + h * HEAD : 3 * WIDE + (h + 1) * HEAD, ts], gs)
            qs = slice(2 * WIDE + h * HEAD, 2 * WIDE + (h + 1) * HEAD)
            to = slice(3 * WIDE + h * HEAD, 3 * WIDE + (h + 1) * HEAD)
            gp[to, rs] = (total * 0.125 * slopes[qs, rs].astype(F32)).astype(BF)
    gp[2 * WIDE : 3 * WIDE, :] = (dv[...] * slopes[WIDE : 2 * WIDE, :].astype(F32)).astype(BF)
    gp[4 * WIDE :, :] = (dk[...] * slopes[3 * WIDE :, :].astype(F32)).astype(BF)

    n, half = PART, PART // 2
    for core in range(2):
        (own, other)[core][...] = gp[:, at(place_of(c, (0, core)))]
        up_part[core * n : core * n + n, :] = gp[:, at(place_of(c, (1, core)))]
        down_part[core * n : core * n + n, :] = gp[:, at(place_of(c, (3, core)))]
        opposite = at(place_of(c, (2, core)))
        far_up[core * half : core * half + half, :] = gp[:half, opposite]
        far_down[core * half : core * half + half, :] = gp[half:, opposite]

    for load in loads:
        load.wait()
    for n in range(4):
        rows = slice(n * BLOCK, (n + 1) * BLOCK)
        part = dot(xn[rows, :], gp[WIDE:, :], NT).astype(BF)
        weights[4 * n : 4 * n + 4, :64, :] = part.reshape(4, 64, 4 * WIDE)
    mix = [dot(gp[:WIDE, :], up[h : h + 512, :], NT).reshape(N_DP, 8, 512) for h in (0, 512)]
    weights[:, 64:, :] = jnp.concatenate(mix, axis=1).astype(BF)


def sum_kernel(recv, project, mixing):
    total = recv[0].astype(F32)
    for d in range(1, N_DP):
        total = total + recv[d].astype(F32)
    project[...] = total[:64]
    mixing[:, :512] = total[64:72]
    mixing[:, 512:] = total[72:]


def join_kernel(ctx, parts, out):
    own = pl.multiple_of(ctx[0] * 8, 8)
    for c in range(N_CTX):
        got = parts[c, pl.ds(own, 8), :]
        for kind in range(4):
            start = kind * D + c * WIDE
            out[:, start : start + WIDE] = got[:, kind * WIDE : (kind + 1) * WIDE]


def rows_kernel(ctx, place, w, w_out, *refs):
    parts, out, (hid, gp) = refs[:10], refs[10], refs[11:]
    back = (place[...] == iota((R, R), 0)).astype(BF)

    @pl.when(pl.program_id(0) == 0)
    def _():
        c = ctx[0]
        n, half = PART, PART // 2
        hidden = [None] * 8
        for core in range(2):
            near = slice(core * n, core * n + n)
            rest = slice(core * half, core * half + half)
            far = [parts[6 + core][rest, :], parts[8 + core][rest, :]]
            got = [
                ((0, core), parts[core][...]),
                ((3, core), parts[2 + core][near, :]),
                ((1, core), parts[4 + core][near, :]),
                ((2, core), jnp.concatenate(far, axis=0)),
            ]
            for rel, part in got:
                src = place_of(c, rel)
                hid[:, at(src)] = dot(back, part[:WIDE, :], NT).astype(BF)
                for kind in range(4):
                    start = (kind + 1) * WIDE
                    gp[at(kind * 8 + src), :] = part[start : start + WIDE, :]

    o = dot(hid[...], w_out[...])
    gx = dot(back, dot(w[...], gp[...]).astype(BF), NT)
    cols = gx.shape[1]
    values = [v.reshape(N_DP, 8, cols) for v in (o, gx)]
    out[...] = jnp.concatenate(values, axis=1).reshape(2 * R, cols).astype(BF)


def unpack_kernel(recv, hist, gout, order, out, grad):
    got = recv[...].astype(F32).reshape(N_DP, 2, 8, D)
    back = (order[...] == iota((R, R), 0)).astype(BF)
    o = dot(back, got[:, 0].reshape(R, D).astype(BF))
    gx = dot(back, got[:, 1].reshape(R, D).astype(BF))
    x = hist[...].astype(F32)
    out[...] = (o + x).astype(BF)
    normed, inverse = row_norm(x)
    first = jnp.mean(gx, axis=-1, keepdims=True)
    second = jnp.mean(gx * normed, axis=-1, keepdims=True)
    grad[...] = (inverse * (gx - first - normed * second) + gout[...].astype(F32)).astype(BF)


def own_weights(ctx_s, w_project):
    return pl.pallas_call(
        own_weights_kernel,
        grid_spec=pltpu.PrefetchScalarGridSpec(
            num_scalar_prefetch=1,
            grid=(4,),
            in_specs=[pl.BlockSpec((D, WIDE), lambda k, ctx: (0, k * N_CTX + ctx[0]))],
            out_specs=pl.BlockSpec((WIDE, D), lambda k, ctx: (k, 0)),
        ),
        out_shape=pltpu.HBM((4 * WIDE, D), BF),
        compiler_params=pltpu.CompilerParams(vmem_limit_bytes=VMEM_BYTES),
    )(ctx_s, w_project)


def own_rows(ctx_s, w_out):
    return pl.pallas_call(
        copy_kernel,
        grid_spec=pltpu.PrefetchScalarGridSpec(
            num_scalar_prefetch=1,
            grid=(1,),
            in_specs=[pl.BlockSpec((WIDE, D), lambda k, ctx: (ctx[0], 0))],
            out_specs=pl.BlockSpec((WIDE, D), lambda k, ctx: (0, 0)),
        ),
        out_shape=pltpu.HBM((WIDE, D), BF),
        compiler_params=pltpu.CompilerParams(vmem_limit_bytes=VMEM_BYTES),
    )(ctx_s, w_out)


def rows_back(ctx_s, place, w_project, w_out, parts, late):
    cols = 256
    whole = pl.BlockSpec(memory_space=pltpu.VMEM)
    return pl.pallas_call(
        skip(rows_kernel, 14, 1),
        grid=(D // cols,),
        in_specs=[
            pl.BlockSpec(memory_space=pltpu.SMEM),
            whole,
            pl.BlockSpec((cols, 4 * D), lambda n: (n, 0)),
            pl.BlockSpec((D, cols), lambda n: (0, n)),
        ]
        + [whole] * 10
        + [pl.BlockSpec(memory_space=pl.ANY)],
        out_specs=pl.BlockSpec((2 * R, cols), lambda n: (0, n)),
        out_shape=pltpu.HBM((2 * R, D), BF),
        scratch_shapes=[pltpu.VMEM((R, D), BF), pltpu.VMEM((4 * D, R), BF)],
        compiler_params=pltpu.CompilerParams(vmem_limit_bytes=VMEM_BYTES),
    )(ctx_s, place, w_project, w_out, *parts, late)


def across(x, axis):
    return lax.all_to_all(x, axis, split_axis=0, concat_axis=0, tiled=True)


def local(history, grad_output, lengths, send_order, place_order, w_project, w_out):
    ctx_s = lax.axis_index("ctx").astype(jnp.int32).reshape(1)
    history, grad_output = hbm(history), hbm(grad_output)
    w_project, w_out = hbm(w_project), hbm(w_out)
    order = send_order.reshape(1, R)
    place = place_order.reshape(1, R)

    (packed,) = call(pack_kernel, [((2 * R, D), BF)], history, grad_output, order)
    w_own, w_out_own = own_weights(ctx_s, w_project), own_rows(ctx_s, w_out)
    arrived = across(packed, "dp")
    (shard,) = call(place_kernel, [((2 * D, R), BF)], arrived, place, late=(w_own, w_out_own))
    xn, up, slopes, proj, att, gh, sums = call(
        forward_kernel,
        [
            ((D, GROUP), BF),
            ((D, GROUP), BF),
            ((4 * WIDE, GROUP), BF),
            ((4 * WIDE, GROUP), BF),
            ((WIDE, GROUP), F32),
            ((WIDE, GROUP), F32),
            ((8, GROUP), F32),
        ],
        lengths,
        ctx_s,
        *[hbm(v) for v in (w_own, w_out_own, *ring_gather(shard))],
        smem=2,
    )
    all_sums = [sums] + [send(sums, step, 0) for step in (2, 1, 3)]
    all_sums += [send(v, 0, 1) for v in all_sums]
    own, other, up_part, down_part, far_up, far_down, weights = call(
        backward_kernel,
        [
            ((PART, R), BF),
            ((PART, R), BF),
            ((2 * PART, R), BF),
            ((2 * PART, R), BF),
            ((PART, R), BF),
            ((PART, R), BF),
            ((N_DP, 80, 4 * WIDE), BF),
        ],
        lengths,
        ctx_s,
        *[hbm(v) for v in (slopes, proj, att, gh)],
        *all_sums,
        hbm(xn),
        hbm(up),
        smem=2,
        plain=2,
        scratch=[
            pltpu.VMEM((PART, GROUP), BF),
            pltpu.VMEM((WIDE, GROUP), BF),
            pltpu.VMEM((WIDE, GROUP), F32),
            pltpu.VMEM((WIDE, GROUP), F32),
            pltpu.VMEM((D, GROUP), BF),
            pltpu.VMEM((D, GROUP), BF),
            pltpu.SemaphoreType.DMA((2,)),
        ],
    )
    parts = relay(own, other, (up_part, down_part), (far_up, far_down))
    project, mixing = call(
        sum_kernel,
        [((64, 4 * WIDE), F32), ((8, D), F32)],
        across(weights, "dp"),
        late=parts[1:],
    )
    owners = [(d * 8 + c, (2 * c + d // 8) * 8 + d % 8) for d in range(N_DP) for c in range(N_CTX)]
    mixing_grad = lax.ppermute(mixing, ("dp", "ctx"), owners)
    project_all = lax.all_gather(project, "ctx")
    rows = rows_back(ctx_s, place, w_project, w_out, parts, project)
    returned = across(rows, "dp")
    output, input_grad = call(
        unpack_kernel, [((R, D), BF), ((R, D), BF)], returned, history, grad_output, order
    )
    (project_grad,) = call(join_kernel, [((8, 4 * D), F32)], ctx_s, project_all, smem=1)
    return output, input_grad, project_grad, mixing_grad


def solution(mesh):
    rows = P(("dp", "ctx"), None)
    ids = P(("dp", "ctx"))
    return jax.shard_map(
        local,
        mesh=mesh,
        in_specs=(rows, rows, P("dp", None), ids, ids, P(), P()),
        out_specs=(rows, rows, rows, rows),
        check_vma=False,
    )
```

```python
import jax
import jax.numpy as jnp
from jax import lax
from jax.experimental import pallas as pl
from jax.experimental.pallas import tpu as pltpu
from jax.sharding import PartitionSpec as P


D = 1024
WIDE = 128
PART = 5 * WIDE
HEAD = 64
N_DP = 16
N_CTX = 8
R = 128
GROUP = 1024
BLOCK = 256
EPS = 1e-6
BF = jnp.bfloat16
F32 = jnp.float32
NN = (((1,), (0,)), ((), ()))
NT = (((1,), (1,)), ((), ()))
VMEM_BYTES = 32 * 1024 * 1024


def dot(a, b, dims=NN):
    return lax.dot_general(a, b, dims, preferred_element_type=F32)


def sigmoid(v):
    return 0.5 * jnp.tanh(0.5 * v) + 0.5


def iota(shape, dim):
    return lax.broadcasted_iota(jnp.int32, shape, dim)


def row_norm(values):
    centred = values - jnp.mean(values, axis=-1, keepdims=True)
    inverse = lax.rsqrt(jnp.mean(centred * centred, axis=-1, keepdims=True) + EPS)
    return centred * inverse, inverse


def skip(body, first, count):
    def kernel(*refs):
        body(*refs[:first], *refs[first + count :])

    return kernel if count else body


def hbm(x):
    return pltpu.with_memory_space_constraint(x, pltpu.HBM)


def call(body, outs, *args, smem=0, plain=0, scratch=(), late=()):
    specs = [pl.BlockSpec(memory_space=pltpu.SMEM)] * smem
    specs += [pl.BlockSpec(memory_space=pltpu.VMEM)] * (len(args) - smem - plain)
    specs += [pl.BlockSpec(memory_space=pl.ANY)] * (plain + len(late))
    return pl.pallas_call(
        skip(body, len(args), len(late)),
        out_shape=[pltpu.HBM(s, t) for s, t in outs],
        in_specs=specs,
        out_specs=[pl.BlockSpec(memory_space=pltpu.VMEM)] * len(outs),
        scratch_shapes=list(scratch),
        compiler_params=pltpu.CompilerParams(vmem_limit_bytes=VMEM_BYTES),
    )(*args, *late)


REL = [(0, 0), (0, 1), (1, 0), (1, 1), (2, 0), (2, 1), (3, 0), (3, 1)]


def place_of(ctx, rel):
    chip = lax.rem((ctx >> 1) + rel[0], 4)
    return chip * 2 + ((ctx & 1) ^ rel[1])


def send(x, step, flip):
    pairs = [(2 * a + b, 2 * ((a + step) % 4) + (b ^ flip)) for a in range(4) for b in range(2)]
    return lax.ppermute(x, "ctx", pairs)


def ring_gather(a, b):
    a_up, b_down = send(a, 3, 0), send(b, 1, 0)
    a_far, b_far = send(a_up, 3, 0), send(b_down, 1, 0)
    b_up, a_down = send(b, 3, 0), send(a, 1, 0)
    got = []
    for v in (a, a_up, a_far, a_down, b, b_up, b_far, b_down):
        got += [v, send(v, 0, 1)]
    return got


def relay(own, other, near, far):
    far = [send(send(far[0], 1, 0), 1, 0), send(send(far[1], 3, 0), 3, 0)]
    near = [send(near[0], 1, 0), send(near[1], 3, 0)]
    got = [own, send(other, 0, 1)]
    for v in near + far:
        got += [v, send(v, 0, 1)]
    return got


def at(index):
    return pl.ds(pl.multiple_of(index * R, R), R)


def copy_kernel(ctx, x, out):
    del ctx
    out[...] = x[...]


def pick_rows(ids):
    return (ids == iota((R, R), 0)).astype(F32).T.astype(BF)


def pack_kernel(hist, gout, order, out):
    xn = row_norm(hist[...].astype(F32))[0].astype(BF)
    pick = pick_rows(order[...])
    a = dot(pick, xn).reshape(N_DP, 8, D)
    b = dot(pick, gout[...]).reshape(N_DP, 8, D)
    out[...] = jnp.concatenate([a, b], axis=1).reshape(2 * R, D).astype(BF)


def own_weights_kernel(ctx, w, out):
    del ctx
    out[...] = w[...].astype(F32).T.astype(BF)


def place_kernel(recv, place, *outs):
    pick = pick_rows(place[...])
    got = recv[...].astype(F32).reshape(N_DP, 2, 8, D)
    for i in range(2):
        rows = dot(pick, got[:, i].reshape(R, D).astype(BF))
        outs[i][...] = rows.T.astype(BF)


def first_visible(lengths):
    rows = iota((1, GROUP), 1)
    low = jnp.full((1, GROUP), 1 << 20, jnp.int32)
    start = jnp.int32(0)
    for j in range(4):
        length = lengths[0, j]
        low = jnp.where((rows >= start) & (rows < start + length), start, low)
        start = start + ((length + 127) >> 7) * 128
    return low


def visible_block(low, rb, tb):
    rs = slice(rb * BLOCK, (rb + 1) * BLOCK)
    keys = iota((BLOCK, BLOCK), 0) + tb * BLOCK
    seen = keys >= low[:, rs]
    if tb == rb:
        seen = seen & (keys <= iota((BLOCK, BLOCK), 1) + rb * BLOCK)
    return seen


def masked_head(x, h, scale=None):
    rows = iota(x.shape, 0)
    x = jnp.where((rows >= h * HEAD) & (rows < (h + 1) * HEAD), x, 0.0)
    if scale is not None:
        x = x * scale
    return x.astype(BF)


def forward_kernel(lengths, ctx, wt, w_out, *refs):
    shards = refs[:16]
    xn, up, slopes, proj, att, gh, sums = refs[16:]
    c = ctx[0]
    for i, rel in enumerate(REL):
        to = at(place_of(c, rel))
        xn[:, to] = shards[i][...]
        up[:, to] = shards[8 + i][...]
    for n in range(GROUP // BLOCK):
        cols = slice(n * BLOCK, (n + 1) * BLOCK)
        p = dot(wt[...], xn[:, cols])
        sig = sigmoid(p)
        out = p * sig
        slopes[:, cols] = (sig + out * (1.0 - sig)).astype(BF)
        proj[:, cols] = out.astype(BF)
        gh[:, cols] = dot(w_out[...], up[:, cols])
    low = first_visible(lengths)
    keys = proj[3 * WIDE :, :].astype(F32).T.astype(BF)
    for rb in range(GROUP // BLOCK):
        rs = slice(rb * BLOCK, (rb + 1) * BLOCK)
        query = proj[2 * WIDE : 3 * WIDE, rs].astype(F32)
        for h in range(2):
            hs = slice(h * HEAD, (h + 1) * HEAD)
            q = masked_head(query, h, 0.125)
            total = jnp.zeros((HEAD, BLOCK), F32)
            for tb in range(rb + 1):
                ts = slice(tb * BLOCK, (tb + 1) * BLOCK)
                s = dot(keys[ts], q)
                w = jnp.where(visible_block(low, rb, tb), s * sigmoid(s), 0.0).astype(BF)
                total = total + dot(proj[WIDE + h * HEAD : WIDE + (h + 1) * HEAD, ts], w)
            att[hs, rs] = total
    a = att[...]
    mean = jnp.mean(a, axis=0, keepdims=True)
    dev = a - mean
    gz = gh[...] * proj[:WIDE, :].astype(F32)
    sums[0:1, :] = mean
    sums[1:2, :] = jnp.sum(dev * dev, axis=0, keepdims=True)
    sums[2:3, :] = jnp.sum(gz, axis=0, keepdims=True)
    sums[3:4, :] = jnp.sum(gz * dev, axis=0, keepdims=True)
    sums[4:8, :] = jnp.zeros((4, GROUP), F32)


def backward_kernel(lengths, ctx, slopes, proj, att, gh, *refs):
    sums, (xn_hbm, up_hbm) = refs[:8], refs[8:10]
    own, other, up_part, down_part, far_up, far_down, weights = refs[10:17]
    gp, gatt, dk, dv, xn, up, sems = refs[17:]
    loads = [
        pltpu.make_async_copy(xn_hbm, xn, sems.at[0]),
        pltpu.make_async_copy(up_hbm, up, sems.at[1]),
    ]
    for load in loads:
        load.start()
    c = ctx[0]
    each = [s[...] for s in sums]
    mean = sum(s[0:1, :] for s in each) * (1.0 / N_CTX)
    spread = sum(s[1:2, :] + WIDE * jnp.square(s[0:1, :] - mean) for s in each)
    inverse = lax.rsqrt(spread * (1.0 / D) + EPS)
    first = sum(s[2:3, :] for s in each) * (1.0 / D)
    second = sum(s[3:4, :] + (s[0:1, :] - mean) * s[2:3, :] for s in each) * inverse * (1.0 / D)
    for n in range(GROUP // BLOCK):
        cols = slice(n * BLOCK, (n + 1) * BLOCK)
        z = (att[:, cols] - mean[:, cols]) * inverse[:, cols]
        gate = proj[:WIDE, cols].astype(F32)
        grad = gh[:, cols]
        gp[:WIDE, cols] = (z * gate).astype(BF)
        gp[WIDE : 2 * WIDE, cols] = (grad * z * slopes[:WIDE, cols].astype(F32)).astype(BF)
        rest = grad * gate - first[:, cols] - z * second[:, cols]
        gatt[:, cols] = (inverse[:, cols] * rest).astype(BF)

    low = first_visible(lengths)
    keys = proj[3 * WIDE :, :].astype(F32).T.astype(BF)
    values = proj[WIDE : 2 * WIDE, :].astype(F32).T.astype(BF)
    dk[...] = jnp.zeros((WIDE, GROUP), F32)
    dv[...] = jnp.zeros((WIDE, GROUP), F32)
    for rb in range(GROUP // BLOCK):
        rs = slice(rb * BLOCK, (rb + 1) * BLOCK)
        query = proj[2 * WIDE : 3 * WIDE, rs].astype(F32)
        grad = gatt[:, rs].astype(F32)
        for h in range(2):
            hs = slice(h * HEAD, (h + 1) * HEAD)
            q = masked_head(query, h, 0.125)
            g = masked_head(grad, h)
            total = jnp.zeros((HEAD, BLOCK), F32)
            for tb in range(rb + 1):
                ts = slice(tb * BLOCK, (tb + 1) * BLOCK)
                s = dot(keys[ts], q)
                gw = dot(values[ts], g)
                seen = visible_block(low, rb, tb)
                sig = sigmoid(s)
                w = jnp.where(seen, s * sig, 0.0)
                gs = jnp.where(seen, gw * (sig + w * (1.0 - sig)), 0.0).astype(BF)
                dv[hs, ts] += dot(g[hs], w.astype(BF), NT)
                dk[hs, ts] += dot(q[hs], gs, NT)
                total = total + dot(proj[3 * WIDE + h * HEAD : 3 * WIDE + (h + 1) * HEAD, ts], gs)
            qs = slice(2 * WIDE + h * HEAD, 2 * WIDE + (h + 1) * HEAD)
            to = slice(3 * WIDE + h * HEAD, 3 * WIDE + (h + 1) * HEAD)
            gp[to, rs] = (total * 0.125 * slopes[qs, rs].astype(F32)).astype(BF)
    gp[2 * WIDE : 3 * WIDE, :] = (dv[...] * slopes[WIDE : 2 * WIDE, :].astype(F32)).astype(BF)
    gp[4 * WIDE :, :] = (dk[...] * slopes[3 * WIDE :, :].astype(F32)).astype(BF)

    n, half = PART, PART // 2
    for core in range(2):
        (own, other)[core][...] = gp[:, at(place_of(c, (0, core)))]
        up_part[core * n : core * n + n, :] = gp[:, at(place_of(c, (1, core)))]
        down_part[core * n : core * n + n, :] = gp[:, at(place_of(c, (3, core)))]
        opposite = at(place_of(c, (2, core)))
        far_up[core * half : core * half + half, :] = gp[:half, opposite]
        far_down[core * half : core * half + half, :] = gp[half:, opposite]

    for load in loads:
        load.wait()
    for n in range(4):
        rows = slice(n * BLOCK, (n + 1) * BLOCK)
        part = dot(xn[rows, :], gp[WIDE:, :], NT).astype(BF)
        weights[4 * n : 4 * n + 4, :64, :] = part.reshape(4, 64, 4 * WIDE)
    mix = [dot(gp[:WIDE, :], up[h : h + 512, :], NT).reshape(N_DP, 8, 512) for h in (0, 512)]
    weights[:, 64:, :] = jnp.concatenate(mix, axis=1).astype(BF)


def sum_kernel(ctx, recv, *refs):
    own, other, chips, mixing, total = refs[0], refs[1], refs[2:5], refs[5], refs[6]
    got = recv[0].astype(F32)
    for d in range(1, N_DP):
        got = got + recv[d].astype(F32)
    total[...] = got[:64]
    mixing[:, :512] = got[64:72]
    mixing[:, 512:] = got[72:]

    def rows(rel):
        return total[pl.ds(pl.multiple_of(place_of(ctx[0], rel) * 8, 8), 8), :]

    own[...] = rows((0, 0))
    other[...] = rows((0, 1))
    for step, part in zip((1, 2, 3), chips):
        part[:8, :] = rows((step, 0))
        part[8:, :] = rows((step, 1))


def join_kernel(ctx, *refs):
    parts, out = refs[:8], refs[8]
    for i, part in enumerate(parts):
        core = i % 2
        src = place_of(ctx[0], ((4 - i // 2) % 4, core))
        got = part[...] if i < 2 else part[core * 8 : core * 8 + 8, :]
        for kind in range(4):
            out[:, at(kind * 8 + src)] = got[:, kind * WIDE : (kind + 1) * WIDE]


def rows_kernel(ctx, place, w, w_out, *refs):
    parts, out, (hid, gp) = refs[:10], refs[10], refs[11:]
    back = (place[...] == iota((R, R), 0)).astype(BF)

    @pl.when(pl.program_id(0) == 0)
    def _():
        c = ctx[0]
        n, half = PART, PART // 2
        hidden = [None] * 8
        for core in range(2):
            near = slice(core * n, core * n + n)
            rest = slice(core * half, core * half + half)
            far = [parts[6 + core][rest, :], parts[8 + core][rest, :]]
            got = [
                ((0, core), parts[core][...]),
                ((3, core), parts[2 + core][near, :]),
                ((1, core), parts[4 + core][near, :]),
                ((2, core), jnp.concatenate(far, axis=0)),
            ]
            for rel, part in got:
                src = place_of(c, rel)
                hid[:, at(src)] = dot(back, part[:WIDE, :], NT).astype(BF)
                for kind in range(4):
                    start = (kind + 1) * WIDE
                    gp[at(kind * 8 + src), :] = part[start : start + WIDE, :]

    o = dot(hid[...], w_out[...])
    gx = dot(back, dot(w[...], gp[...]).astype(BF), NT)
    cols = gx.shape[1]
    values = [v.reshape(N_DP, 8, cols) for v in (o, gx)]
    out[...] = jnp.concatenate(values, axis=1).reshape(2 * R, cols).astype(BF)


def unpack_kernel(recv, hist, gout, order, out, grad):
    got = recv[...].astype(F32).reshape(N_DP, 2, 8, D)
    back = (order[...] == iota((R, R), 0)).astype(BF)
    o = dot(back, got[:, 0].reshape(R, D).astype(BF))
    gx = dot(back, got[:, 1].reshape(R, D).astype(BF))
    x = hist[...].astype(F32)
    out[...] = (o + x).astype(BF)
    normed, inverse = row_norm(x)
    first = jnp.mean(gx, axis=-1, keepdims=True)
    second = jnp.mean(gx * normed, axis=-1, keepdims=True)
    grad[...] = (inverse * (gx - first - normed * second) + gout[...].astype(F32)).astype(BF)


def own_weights(ctx_s, w_project):
    return pl.pallas_call(
        own_weights_kernel,
        grid_spec=pltpu.PrefetchScalarGridSpec(
            num_scalar_prefetch=1,
            grid=(4,),
            in_specs=[pl.BlockSpec((D, WIDE), lambda k, ctx: (0, k * N_CTX + ctx[0]))],
            out_specs=pl.BlockSpec((WIDE, D), lambda k, ctx: (k, 0)),
        ),
        out_shape=pltpu.HBM((4 * WIDE, D), BF),
        compiler_params=pltpu.CompilerParams(vmem_limit_bytes=VMEM_BYTES),
    )(ctx_s, w_project)


def own_rows(ctx_s, w_out):
    return pl.pallas_call(
        copy_kernel,
        grid_spec=pltpu.PrefetchScalarGridSpec(
            num_scalar_prefetch=1,
            grid=(1,),
            in_specs=[pl.BlockSpec((WIDE, D), lambda k, ctx: (ctx[0], 0))],
            out_specs=pl.BlockSpec((WIDE, D), lambda k, ctx: (0, 0)),
        ),
        out_shape=pltpu.HBM((WIDE, D), BF),
        compiler_params=pltpu.CompilerParams(vmem_limit_bytes=VMEM_BYTES),
    )(ctx_s, w_out)


def rows_back(ctx_s, place, w_project, w_out, parts, late):
    cols = 256
    whole = pl.BlockSpec(memory_space=pltpu.VMEM)
    return pl.pallas_call(
        skip(rows_kernel, 14, 1),
        grid=(D // cols,),
        in_specs=[
            pl.BlockSpec(memory_space=pltpu.SMEM),
            whole,
            pl.BlockSpec((cols, 4 * D), lambda n: (n, 0)),
            pl.BlockSpec((D, cols), lambda n: (0, n)),
        ]
        + [whole] * 10
        + [pl.BlockSpec(memory_space=pl.ANY)],
        out_specs=pl.BlockSpec((2 * R, cols), lambda n: (0, n)),
        out_shape=pltpu.HBM((2 * R, D), BF),
        scratch_shapes=[pltpu.VMEM((R, D), BF), pltpu.VMEM((4 * D, R), BF)],
        compiler_params=pltpu.CompilerParams(vmem_limit_bytes=VMEM_BYTES),
    )(ctx_s, place, w_project, w_out, *parts, late)


def across(x, axis):
    return lax.all_to_all(x, axis, split_axis=0, concat_axis=0, tiled=True)


def local(history, grad_output, lengths, send_order, place_order, w_project, w_out):
    ctx_s = lax.axis_index("ctx").astype(jnp.int32).reshape(1)
    w_project, w_out = hbm(w_project), hbm(w_out)
    order = send_order.reshape(1, R)
    place = place_order.reshape(1, R)

    (packed,) = call(pack_kernel, [((2 * R, D), BF)], hbm(history), hbm(grad_output), order)
    w_own, w_out_own = own_weights(ctx_s, w_project), own_rows(ctx_s, w_out)
    arrived = across(packed, "dp")
    shard = call(place_kernel, [((D, R), BF)] * 2, arrived, place, late=(w_own, w_out_own))
    xn, up, slopes, proj, att, gh, sums = call(
        forward_kernel,
        [
            ((D, GROUP), BF),
            ((D, GROUP), BF),
            ((4 * WIDE, GROUP), BF),
            ((4 * WIDE, GROUP), BF),
            ((WIDE, GROUP), F32),
            ((WIDE, GROUP), F32),
            ((8, GROUP), F32),
        ],
        lengths,
        ctx_s,
        w_own,
        w_out_own,
        *[hbm(v) for v in ring_gather(*shard)],
        smem=2,
    )
    all_sums = [sums] + [send(sums, step, 0) for step in (2, 1, 3)]
    all_sums += [send(v, 0, 1) for v in all_sums]
    own, other, up_part, down_part, far_up, far_down, weights = call(
        backward_kernel,
        [
            ((PART, R), BF),
            ((PART, R), BF),
            ((2 * PART, R), BF),
            ((2 * PART, R), BF),
            ((PART, R), BF),
            ((PART, R), BF),
            ((N_DP, 80, 4 * WIDE), BF),
        ],
        lengths,
        ctx_s,
        *[hbm(v) for v in (slopes, proj, att, gh)],
        *all_sums,
        hbm(xn),
        hbm(up),
        smem=2,
        plain=2,
        scratch=[
            pltpu.VMEM((PART, GROUP), BF),
            pltpu.VMEM((WIDE, GROUP), BF),
            pltpu.VMEM((WIDE, GROUP), F32),
            pltpu.VMEM((WIDE, GROUP), F32),
            pltpu.VMEM((D, GROUP), BF),
            pltpu.VMEM((D, GROUP), BF),
            pltpu.SemaphoreType.DMA((2,)),
        ],
    )
    parts = relay(own, other, (up_part, down_part), (far_up, far_down))
    own, other, *chips, mixing = call(
        sum_kernel,
        [((8, 4 * WIDE), F32)] * 2 + [((16, 4 * WIDE), F32)] * 3 + [((8, D), F32)],
        ctx_s,
        across(weights, "dp"),
        smem=1,
        late=parts[1:],
        scratch=[pltpu.VMEM((64, 4 * WIDE), F32)],
    )
    owners = [(d * 8 + c, (2 * c + d // 8) * 8 + d % 8) for d in range(N_DP) for c in range(N_CTX)]
    mixing_grad = lax.ppermute(mixing, ("dp", "ctx"), owners)
    project = [own, send(other, 0, 1)]
    for step, part in zip((1, 2, 3), chips):
        part = send(part, step, 0)
        project += [part, send(part, 0, 1)]
    rows = rows_back(ctx_s, place, w_project, w_out, parts, own)
    returned = across(rows, "dp")
    output, input_grad = call(
        unpack_kernel, [((R, D), BF), ((R, D), BF)], returned, history, grad_output, order
    )
    (project_grad,) = call(join_kernel, [((8, 4 * D), F32)], ctx_s, *project, smem=1)
    return output, input_grad, project_grad, mixing_grad


def solution(mesh):
    rows = P(("dp", "ctx"), None)
    ids = P(("dp", "ctx"))
    return jax.shard_map(
        local,
        mesh=mesh,
        in_specs=(rows, rows, P("dp", None), ids, ids, P(), P()),
        out_specs=(rows, rows, rows, rows),
        check_vma=False,
    )
```

```python
import jax
import jax.numpy as jnp
from jax import lax
from jax.experimental import pallas as pl
from jax.experimental.pallas import tpu as pltpu
from jax.sharding import PartitionSpec as P


D = 1024
WIDE = 128
PART = 5 * WIDE
HEAD = 64
N_DP = 16
N_CTX = 8
R = 128
GROUP = 1024
BLOCK = 256
EPS = 1e-6
BF = jnp.bfloat16
F32 = jnp.float32
NN = (((1,), (0,)), ((), ()))
NT = (((1,), (1,)), ((), ()))
VMEM_BYTES = 32 * 1024 * 1024


def dot(a, b, dims=NN):
    return lax.dot_general(a, b, dims, preferred_element_type=F32)


def sigmoid(v):
    return 0.5 * jnp.tanh(0.5 * v) + 0.5


def iota(shape, dim):
    return lax.broadcasted_iota(jnp.int32, shape, dim)


def row_norm(values):
    centred = values - jnp.mean(values, axis=-1, keepdims=True)
    inverse = lax.rsqrt(jnp.mean(centred * centred, axis=-1, keepdims=True) + EPS)
    return centred * inverse, inverse


def skip(body, first, count):
    def kernel(*refs):
        body(*refs[:first], *refs[first + count :])

    return kernel if count else body


def hbm(x):
    return pltpu.with_memory_space_constraint(x, pltpu.HBM)


def call(body, outs, *args, smem=0, plain=0, plain_outs=0, scratch=(), late=()):
    specs = [pl.BlockSpec(memory_space=pltpu.SMEM)] * smem
    specs += [pl.BlockSpec(memory_space=pltpu.VMEM)] * (len(args) - smem - plain)
    specs += [pl.BlockSpec(memory_space=pl.ANY)] * (plain + len(late))
    return pl.pallas_call(
        skip(body, len(args), len(late)),
        out_shape=[pltpu.HBM(s, t) for s, t in outs],
        in_specs=specs,
        out_specs=[pl.BlockSpec(memory_space=pl.ANY)] * plain_outs
        + [pl.BlockSpec(memory_space=pltpu.VMEM)] * (len(outs) - plain_outs),
        scratch_shapes=list(scratch),
        compiler_params=pltpu.CompilerParams(vmem_limit_bytes=VMEM_BYTES),
    )(*args, *late)


REL = [(0, 0), (0, 1), (1, 0), (1, 1), (2, 0), (2, 1), (3, 0), (3, 1)]


def place_of(ctx, rel):
    chip = lax.rem((ctx >> 1) + rel[0], 4)
    return chip * 2 + ((ctx & 1) ^ rel[1])


def send(x, step, flip):
    pairs = [(2 * a + b, 2 * ((a + step) % 4) + (b ^ flip)) for a in range(4) for b in range(2)]
    return lax.ppermute(x, "ctx", pairs)


def ring_gather(a, b):
    a_up, b_down = send(a, 3, 0), send(b, 1, 0)
    a_far, b_far = send(a_up, 3, 0), send(b_down, 1, 0)
    b_up, a_down = send(b, 3, 0), send(a, 1, 0)
    got = []
    for v in (a, a_up, a_far, a_down, b, b_up, b_far, b_down):
        got += [v, send(v, 0, 1)]
    return got


def relay(own, other, near, far):
    far = [send(send(far[0], 1, 0), 1, 0), send(send(far[1], 3, 0), 3, 0)]
    near = [send(near[0], 1, 0), send(near[1], 3, 0)]
    got = [own, send(other, 0, 1)]
    for v in near + far:
        got += [v, send(v, 0, 1)]
    return got


def at(index):
    return pl.ds(pl.multiple_of(index * R, R), R)


def copy_kernel(ctx, x, out):
    del ctx
    out[...] = x[...]


def pick_rows(ids):
    return (ids == iota((R, R), 0)).astype(F32).T.astype(BF)


def pack_kernel(hist, gout, order, out):
    xn = row_norm(hist[...].astype(F32))[0].astype(BF)
    pick = pick_rows(order[...])
    a = dot(pick, xn).reshape(N_DP, 8, D)
    b = dot(pick, gout[...]).reshape(N_DP, 8, D)
    out[...] = jnp.concatenate([a, b], axis=1).reshape(2 * R, D).astype(BF)


def own_weights_kernel(ctx, w, out):
    del ctx
    out[...] = w[...].astype(F32).T.astype(BF)


def place_kernel(recv, place, *outs):
    pick = pick_rows(place[...])
    got = recv[...].astype(F32).reshape(N_DP, 2, 8, D)
    for i in range(2):
        rows = dot(pick, got[:, i].reshape(R, D).astype(BF))
        outs[i][...] = rows.T.astype(BF)


def first_visible(lengths):
    rows = iota((1, GROUP), 1)
    low = jnp.full((1, GROUP), 1 << 20, jnp.int32)
    start = jnp.int32(0)
    for j in range(4):
        length = lengths[0, j]
        low = jnp.where((rows >= start) & (rows < start + length), start, low)
        start = start + ((length + 127) >> 7) * 128
    return low


def visible_block(low, rb, tb):
    rs = slice(rb * BLOCK, (rb + 1) * BLOCK)
    keys = iota((BLOCK, BLOCK), 0) + tb * BLOCK
    seen = keys >= low[:, rs]
    if tb == rb:
        seen = seen & (keys <= iota((BLOCK, BLOCK), 1) + rb * BLOCK)
    return seen


def masked_head(x, h, scale=None):
    rows = iota(x.shape, 0)
    x = jnp.where((rows >= h * HEAD) & (rows < (h + 1) * HEAD), x, 0.0)
    if scale is not None:
        x = x * scale
    return x.astype(BF)


def shard_loads(c, shards, xn, up, sems):
    loads = []
    for i, rel in enumerate(REL):
        to = at(place_of(c, rel))
        loads.append(pltpu.make_async_copy(shards[i], xn.at[:, to], sems.at[i]))
        loads.append(pltpu.make_async_copy(shards[8 + i], up.at[:, to], sems.at[8 + i]))
    return loads


def forward_kernel(lengths, ctx, wt, w_out, *refs):
    shards, results, (att, sums) = refs[:16], refs[16:19], refs[19:21]
    xn, up, slopes, proj, gh, sems, out_sems = refs[21:]
    loads = shard_loads(ctx[0], shards, xn, up, sems)
    for load in loads:
        load.start()
    for load in loads:
        load.wait()
    for n in range(GROUP // BLOCK):
        cols = slice(n * BLOCK, (n + 1) * BLOCK)
        p = dot(wt[...], xn[:, cols])
        sig = sigmoid(p)
        out = p * sig
        slopes[:, cols] = (sig + out * (1.0 - sig)).astype(BF)
        proj[:, cols] = out.astype(BF)
        gh[:, cols] = dot(w_out[...], up[:, cols])
    stores = [
        pltpu.make_async_copy(v, out, out_sems.at[i])
        for i, (v, out) in enumerate(zip((slopes, proj, gh), results))
    ]
    for store in stores:
        store.start()
    low = first_visible(lengths)
    keys = proj[3 * WIDE :, :].astype(F32).T.astype(BF)
    for rb in range(GROUP // BLOCK):
        rs = slice(rb * BLOCK, (rb + 1) * BLOCK)
        query = proj[2 * WIDE : 3 * WIDE, rs].astype(F32)
        for h in range(2):
            hs = slice(h * HEAD, (h + 1) * HEAD)
            q = masked_head(query, h, 0.125)
            total = jnp.zeros((HEAD, BLOCK), F32)
            for tb in range(rb + 1):
                ts = slice(tb * BLOCK, (tb + 1) * BLOCK)
                s = dot(keys[ts], q)
                w = jnp.where(visible_block(low, rb, tb), s * sigmoid(s), 0.0).astype(BF)
                total = total + dot(proj[WIDE + h * HEAD : WIDE + (h + 1) * HEAD, ts], w)
            att[hs, rs] = total
    a = att[...]
    mean = jnp.mean(a, axis=0, keepdims=True)
    dev = a - mean
    gz = gh[...] * proj[:WIDE, :].astype(F32)
    sums[0:1, :] = mean
    sums[1:2, :] = jnp.sum(dev * dev, axis=0, keepdims=True)
    sums[2:3, :] = jnp.sum(gz, axis=0, keepdims=True)
    sums[3:4, :] = jnp.sum(gz * dev, axis=0, keepdims=True)
    sums[4:8, :] = jnp.zeros((4, GROUP), F32)
    for store in stores:
        store.wait()


def backward_kernel(lengths, ctx, slopes, proj, att, gh, *refs):
    sums, shards = refs[:8], refs[8:24]
    own, other, up_part, down_part, far_up, far_down, weights = refs[24:31]
    gp, gatt, dk, dv, xn, up, sems, out_sems = refs[31:]
    c = ctx[0]
    loads = shard_loads(c, shards, xn, up, sems)
    for load in loads:
        load.start()
    each = [s[...] for s in sums]
    mean = sum(s[0:1, :] for s in each) * (1.0 / N_CTX)
    spread = sum(s[1:2, :] + WIDE * jnp.square(s[0:1, :] - mean) for s in each)
    inverse = lax.rsqrt(spread * (1.0 / D) + EPS)
    first = sum(s[2:3, :] for s in each) * (1.0 / D)
    second = sum(s[3:4, :] + (s[0:1, :] - mean) * s[2:3, :] for s in each) * inverse * (1.0 / D)
    for n in range(GROUP // BLOCK):
        cols = slice(n * BLOCK, (n + 1) * BLOCK)
        z = (att[:, cols] - mean[:, cols]) * inverse[:, cols]
        gate = proj[:WIDE, cols].astype(F32)
        grad = gh[:, cols]
        gp[:WIDE, cols] = (z * gate).astype(BF)
        gp[WIDE : 2 * WIDE, cols] = (grad * z * slopes[:WIDE, cols].astype(F32)).astype(BF)
        rest = grad * gate - first[:, cols] - z * second[:, cols]
        gatt[:, cols] = (inverse[:, cols] * rest).astype(BF)

    low = first_visible(lengths)
    keys = proj[3 * WIDE :, :].astype(F32).T.astype(BF)
    values = proj[WIDE : 2 * WIDE, :].astype(F32).T.astype(BF)
    dk[...] = jnp.zeros((WIDE, GROUP), F32)
    dv[...] = jnp.zeros((WIDE, GROUP), F32)
    for rb in range(GROUP // BLOCK):
        rs = slice(rb * BLOCK, (rb + 1) * BLOCK)
        query = proj[2 * WIDE : 3 * WIDE, rs].astype(F32)
        grad = gatt[:, rs].astype(F32)
        for h in range(2):
            hs = slice(h * HEAD, (h + 1) * HEAD)
            q = masked_head(query, h, 0.125)
            g = masked_head(grad, h)
            total = jnp.zeros((HEAD, BLOCK), F32)
            for tb in range(rb + 1):
                ts = slice(tb * BLOCK, (tb + 1) * BLOCK)
                s = dot(keys[ts], q)
                gw = dot(values[ts], g)
                seen = visible_block(low, rb, tb)
                sig = sigmoid(s)
                w = jnp.where(seen, s * sig, 0.0)
                gs = jnp.where(seen, gw * (sig + w * (1.0 - sig)), 0.0).astype(BF)
                dv[hs, ts] += dot(g[hs], w.astype(BF), NT)
                dk[hs, ts] += dot(q[hs], gs, NT)
                total = total + dot(proj[3 * WIDE + h * HEAD : 3 * WIDE + (h + 1) * HEAD, ts], gs)
            qs = slice(2 * WIDE + h * HEAD, 2 * WIDE + (h + 1) * HEAD)
            to = slice(3 * WIDE + h * HEAD, 3 * WIDE + (h + 1) * HEAD)
            gp[to, rs] = (total * 0.125 * slopes[qs, rs].astype(F32)).astype(BF)
    gp[2 * WIDE : 3 * WIDE, :] = (dv[...] * slopes[WIDE : 2 * WIDE, :].astype(F32)).astype(BF)
    gp[4 * WIDE :, :] = (dk[...] * slopes[3 * WIDE :, :].astype(F32)).astype(BF)

    n, half = PART, PART // 2
    moves = []
    for core in range(2):
        opposite = gp.at[:, at(place_of(c, (2, core)))]
        mine = pl.ds(core * half, half)
        moves += [
            (gp.at[:, at(place_of(c, (0, core)))], (own, other)[core]),
            (gp.at[:, at(place_of(c, (1, core)))], up_part.at[pl.ds(core * n, n), :]),
            (gp.at[:, at(place_of(c, (3, core)))], down_part.at[pl.ds(core * n, n), :]),
            (opposite.at[pl.ds(0, half), :], far_up.at[mine, :]),
            (opposite.at[pl.ds(half, half), :], far_down.at[mine, :]),
        ]
    stores = [pltpu.make_async_copy(*m, out_sems.at[i]) for i, m in enumerate(moves)]
    for store in stores:
        store.start()

    for load in loads:
        load.wait()
    for n in range(4):
        rows = slice(n * BLOCK, (n + 1) * BLOCK)
        part = dot(xn[rows, :], gp[WIDE:, :], NT).astype(BF)
        weights[4 * n : 4 * n + 4, :64, :] = part.reshape(4, 64, 4 * WIDE)
    mix = [dot(gp[:WIDE, :], up[h : h + 512, :], NT).reshape(N_DP, 8, 512) for h in (0, 512)]
    weights[:, 64:, :] = jnp.concatenate(mix, axis=1).astype(BF)
    for store in stores:
        store.wait()


def sum_kernel(ctx, recv, *refs):
    own, other, chips, mixing, total = refs[0], refs[1], refs[2:5], refs[5], refs[6]
    got = recv[0].astype(F32)
    for d in range(1, N_DP):
        got = got + recv[d].astype(F32)
    total[...] = got[:64]
    mixing[:, :512] = got[64:72]
    mixing[:, 512:] = got[72:]

    def rows(rel):
        return total[pl.ds(pl.multiple_of(place_of(ctx[0], rel) * 8, 8), 8), :]

    own[...] = rows((0, 0))
    other[...] = rows((0, 1))
    for step, part in zip((1, 2, 3), chips):
        part[:8, :] = rows((step, 0))
        part[8:, :] = rows((step, 1))


def join_kernel(ctx, mixing, *refs):
    parts, out, mixing_out = refs[:8], refs[8], refs[9]
    mixing_out[...] = mixing[...]
    for i, part in enumerate(parts):
        core = i % 2
        src = place_of(ctx[0], ((4 - i // 2) % 4, core))
        got = part[...] if i < 2 else part[core * 8 : core * 8 + 8, :]
        for kind in range(4):
            out[:, at(kind * 8 + src)] = got[:, kind * WIDE : (kind + 1) * WIDE]


def rows_kernel(ctx, place, w, w_out, *refs):
    parts, out, (hid, gp) = refs[:10], refs[10], refs[11:]
    back = (place[...] == iota((R, R), 0)).astype(BF)

    @pl.when(pl.program_id(0) == 0)
    def _():
        c = ctx[0]
        n, half = PART, PART // 2
        hidden = [None] * 8
        for core in range(2):
            near = slice(core * n, core * n + n)
            rest = slice(core * half, core * half + half)
            far = [parts[6 + core][rest, :], parts[8 + core][rest, :]]
            got = [
                ((0, core), parts[core][...]),
                ((3, core), parts[2 + core][near, :]),
                ((1, core), parts[4 + core][near, :]),
                ((2, core), jnp.concatenate(far, axis=0)),
            ]
            for rel, part in got:
                src = place_of(c, rel)
                hid[:, at(src)] = dot(back, part[:WIDE, :], NT).astype(BF)
                for kind in range(4):
                    start = (kind + 1) * WIDE
                    gp[at(kind * 8 + src), :] = part[start : start + WIDE, :]

    o = dot(hid[...], w_out[...])
    gx = dot(back, dot(w[...], gp[...]).astype(BF), NT)
    cols = gx.shape[1]
    values = [v.reshape(N_DP, 8, cols) for v in (o, gx)]
    out[...] = jnp.concatenate(values, axis=1).reshape(2 * R, cols).astype(BF)


def unpack_kernel(recv, hist, gout, order, out, grad):
    got = recv[...].astype(F32).reshape(N_DP, 2, 8, D)
    back = (order[...] == iota((R, R), 0)).astype(BF)
    o = dot(back, got[:, 0].reshape(R, D).astype(BF))
    gx = dot(back, got[:, 1].reshape(R, D).astype(BF))
    x = hist[...].astype(F32)
    out[...] = (o + x).astype(BF)
    normed, inverse = row_norm(x)
    first = jnp.mean(gx, axis=-1, keepdims=True)
    second = jnp.mean(gx * normed, axis=-1, keepdims=True)
    grad[...] = (inverse * (gx - first - normed * second) + gout[...].astype(F32)).astype(BF)


def own_weights(ctx_s, w_project):
    return pl.pallas_call(
        own_weights_kernel,
        grid_spec=pltpu.PrefetchScalarGridSpec(
            num_scalar_prefetch=1,
            grid=(4,),
            in_specs=[pl.BlockSpec((D, WIDE), lambda k, ctx: (0, k * N_CTX + ctx[0]))],
            out_specs=pl.BlockSpec((WIDE, D), lambda k, ctx: (k, 0)),
        ),
        out_shape=pltpu.HBM((4 * WIDE, D), BF),
        compiler_params=pltpu.CompilerParams(vmem_limit_bytes=VMEM_BYTES),
    )(ctx_s, w_project)


def own_rows(ctx_s, w_out):
    return pl.pallas_call(
        copy_kernel,
        grid_spec=pltpu.PrefetchScalarGridSpec(
            num_scalar_prefetch=1,
            grid=(1,),
            in_specs=[pl.BlockSpec((WIDE, D), lambda k, ctx: (ctx[0], 0))],
            out_specs=pl.BlockSpec((WIDE, D), lambda k, ctx: (0, 0)),
        ),
        out_shape=pltpu.HBM((WIDE, D), BF),
        compiler_params=pltpu.CompilerParams(vmem_limit_bytes=VMEM_BYTES),
    )(ctx_s, w_out)


def rows_back(ctx_s, place, w_project, w_out, parts):
    cols = 512
    whole = pl.BlockSpec(memory_space=pltpu.VMEM)
    return pl.pallas_call(
        rows_kernel,
        grid=(D // cols,),
        in_specs=[
            pl.BlockSpec(memory_space=pltpu.SMEM),
            whole,
            pl.BlockSpec((cols, 4 * D), lambda n: (n, 0)),
            pl.BlockSpec((D, cols), lambda n: (0, n)),
        ]
        + [whole] * 10,
        out_specs=pl.BlockSpec((2 * R, cols), lambda n: (0, n)),
        out_shape=pltpu.HBM((2 * R, D), BF),
        scratch_shapes=[pltpu.VMEM((R, D), BF), pltpu.VMEM((4 * D, R), BF)],
        compiler_params=pltpu.CompilerParams(vmem_limit_bytes=VMEM_BYTES),
    )(ctx_s, place, w_project, w_out, *parts)


def across(x, axis):
    return lax.all_to_all(x, axis, split_axis=0, concat_axis=0, tiled=True)


def local(history, grad_output, lengths, send_order, place_order, w_project, w_out):
    ctx_s = lax.axis_index("ctx").astype(jnp.int32).reshape(1)
    w_project, w_out = hbm(w_project), hbm(w_out)
    order = send_order.reshape(1, R)
    place = place_order.reshape(1, R)

    (packed,) = call(pack_kernel, [((2 * R, D), BF)], hbm(history), hbm(grad_output), order)
    w_own, w_out_own = own_weights(ctx_s, w_project), own_rows(ctx_s, w_out)
    arrived = across(packed, "dp")
    shard = call(place_kernel, [((D, R), BF)] * 2, arrived, place, late=(w_own, w_out_own))
    shards = [hbm(v) for v in ring_gather(*shard)]
    slopes, proj, gh, att, sums = call(
        forward_kernel,
        [
            ((4 * WIDE, GROUP), BF),
            ((4 * WIDE, GROUP), BF),
            ((WIDE, GROUP), F32),
            ((WIDE, GROUP), F32),
            ((8, GROUP), F32),
        ],
        lengths,
        ctx_s,
        w_own,
        w_out_own,
        *shards,
        smem=2,
        plain=16,
        plain_outs=3,
        scratch=[
            pltpu.VMEM((D, GROUP), BF),
            pltpu.VMEM((D, GROUP), BF),
            pltpu.VMEM((4 * WIDE, GROUP), BF),
            pltpu.VMEM((4 * WIDE, GROUP), BF),
            pltpu.VMEM((WIDE, GROUP), F32),
            pltpu.SemaphoreType.DMA((16,)),
            pltpu.SemaphoreType.DMA((3,)),
        ],
    )
    all_sums = [sums] + [send(sums, step, 0) for step in (2, 1, 3)]
    all_sums += [send(v, 0, 1) for v in all_sums]
    own, other, up_part, down_part, far_up, far_down, weights = call(
        backward_kernel,
        [
            ((PART, R), BF),
            ((PART, R), BF),
            ((2 * PART, R), BF),
            ((2 * PART, R), BF),
            ((PART, R), BF),
            ((PART, R), BF),
            ((N_DP, 80, 4 * WIDE), BF),
        ],
        lengths,
        ctx_s,
        *[hbm(v) for v in (slopes, proj, att, gh)],
        *all_sums,
        *shards,
        smem=2,
        plain=16,
        plain_outs=6,
        scratch=[
            pltpu.VMEM((PART, GROUP), BF),
            pltpu.VMEM((WIDE, GROUP), BF),
            pltpu.VMEM((WIDE, GROUP), F32),
            pltpu.VMEM((WIDE, GROUP), F32),
            pltpu.VMEM((D, GROUP), BF),
            pltpu.VMEM((D, GROUP), BF),
            pltpu.SemaphoreType.DMA((16,)),
            pltpu.SemaphoreType.DMA((10,)),
        ],
    )
    parts = relay(own, other, (up_part, down_part), (far_up, far_down))
    weights = across(weights, "dp")
    rows = rows_back(ctx_s, place, w_project, w_out, parts)
    own, other, *chips, mixing = call(
        sum_kernel,
        [((8, 4 * WIDE), F32)] * 2 + [((16, 4 * WIDE), F32)] * 3 + [((8, D), F32)],
        ctx_s,
        weights,
        smem=1,
        late=(rows,),
        scratch=[pltpu.VMEM((64, 4 * WIDE), F32)],
    )
    owners = [(d * 8 + c, (2 * c + d // 8) * 8 + d % 8) for d in range(N_DP) for c in range(N_CTX)]
    mixing = lax.ppermute(mixing, ("dp", "ctx"), owners)
    project = [own, send(other, 0, 1)]
    for step, part in zip((1, 2, 3), chips):
        part = send(part, step, 0)
        project += [part, send(part, 0, 1)]
    returned = across(rows, "dp")
    output, input_grad = call(
        unpack_kernel, [((R, D), BF), ((R, D), BF)], returned, history, grad_output, order
    )
    project_grad, mixing_grad = call(
        join_kernel, [((8, 4 * D), F32), ((8, D), F32)], ctx_s, mixing, *project, smem=1
    )
    return output, input_grad, project_grad, mixing_grad


def solution(mesh):
    rows = P(("dp", "ctx"), None)
    ids = P(("dp", "ctx"))
    return jax.shard_map(
        local,
        mesh=mesh,
        in_specs=(rows, rows, P("dp", None), ids, ids, P(), P()),
        out_specs=(rows, rows, rows, rows),
        check_vma=False,
    )
```

```python
import jax
import jax.numpy as jnp
from jax import lax
from jax.experimental import pallas as pl
from jax.experimental.pallas import tpu as pltpu
from jax.sharding import PartitionSpec as P


D = 1024
WIDE = 128
PART = 5 * WIDE
HEAD = 64
N_DP = 16
N_CTX = 8
R = 128
GROUP = 1024
BLOCK = 256
EPS = 1e-6
BF = jnp.bfloat16
F32 = jnp.float32
NN = (((1,), (0,)), ((), ()))
NT = (((1,), (1,)), ((), ()))
VMEM_BYTES = 32 * 1024 * 1024


def dot(a, b, dims=NN):
    return lax.dot_general(a, b, dims, preferred_element_type=F32)


def sigmoid(v):
    return 0.5 * jnp.tanh(0.5 * v) + 0.5


def iota(shape, dim):
    return lax.broadcasted_iota(jnp.int32, shape, dim)


def row_norm(values):
    centred = values - jnp.mean(values, axis=-1, keepdims=True)
    inverse = lax.rsqrt(jnp.mean(centred * centred, axis=-1, keepdims=True) + EPS)
    return centred * inverse, inverse


def skip(body, first, count):
    def kernel(*refs):
        body(*refs[:first], *refs[first + count :])

    return kernel if count else body


def hbm(x):
    return pltpu.with_memory_space_constraint(x, pltpu.HBM)


def call(body, outs, *args, smem=0, plain=0, plain_outs=0, scratch=(), late=()):
    specs = [pl.BlockSpec(memory_space=pltpu.SMEM)] * smem
    specs += [pl.BlockSpec(memory_space=pltpu.VMEM)] * (len(args) - smem - plain)
    specs += [pl.BlockSpec(memory_space=pl.ANY)] * (plain + len(late))
    return pl.pallas_call(
        skip(body, len(args), len(late)),
        out_shape=[pltpu.HBM(s, t) for s, t in outs],
        in_specs=specs,
        out_specs=[pl.BlockSpec(memory_space=pl.ANY)] * plain_outs
        + [pl.BlockSpec(memory_space=pltpu.VMEM)] * (len(outs) - plain_outs),
        scratch_shapes=list(scratch),
        compiler_params=pltpu.CompilerParams(vmem_limit_bytes=VMEM_BYTES),
    )(*args, *late)


REL = [(0, 0), (0, 1), (1, 0), (1, 1), (2, 0), (2, 1), (3, 0), (3, 1)]


def place_of(ctx, rel):
    chip = lax.rem((ctx >> 1) + rel[0], 4)
    return chip * 2 + ((ctx & 1) ^ rel[1])


def send(x, step, flip):
    pairs = [(2 * a + b, 2 * ((a + step) % 4) + (b ^ flip)) for a in range(4) for b in range(2)]
    return lax.ppermute(x, "ctx", pairs)


def ring_gather(a, b):
    a_up, b_down = send(a, 3, 0), send(b, 1, 0)
    a_far, b_far = send(a_up, 3, 0), send(b_down, 1, 0)
    b_up, a_down = send(b, 3, 0), send(a, 1, 0)
    got = []
    for v in (a, a_up, a_far, a_down, b, b_up, b_far, b_down):
        got += [v, send(v, 0, 1)]
    return got


def relay(own, other, near, far):
    far = [send(send(far[0], 1, 0), 1, 0), send(far[1], 2, 0)]
    near = [send(near[0], 1, 0), send(near[1], 3, 0)]
    got = [own, send(other, 0, 1)]
    for v in near + far:
        got += [v, send(v, 0, 1)]
    return got


def at(index):
    return pl.ds(pl.multiple_of(index * R, R), R)


def copy_kernel(ctx, x, out):
    del ctx
    out[...] = x[...]


def pick_rows(ids):
    return (ids == iota((R, R), 0)).astype(F32).T.astype(BF)


def pack_kernel(hist, gout, order, out):
    xn = row_norm(hist[...].astype(F32))[0].astype(BF)
    pick = pick_rows(order[...])
    a = dot(pick, xn).reshape(N_DP, 8, D)
    b = dot(pick, gout[...]).reshape(N_DP, 8, D)
    out[...] = jnp.concatenate([a, b], axis=1).reshape(2 * R, D).astype(BF)


def own_weights_kernel(ctx, w, out):
    del ctx
    out[...] = w[...].astype(F32).T.astype(BF)


def place_kernel(recv, place, *outs):
    pick = pick_rows(place[...])
    got = recv[...].astype(F32).reshape(N_DP, 2, 8, D)
    for i in range(2):
        rows = dot(pick, got[:, i].reshape(R, D).astype(BF))
        outs[i][...] = rows.T.astype(BF)


def first_visible(lengths):
    rows = iota((1, GROUP), 1)
    low = jnp.full((1, GROUP), 1 << 20, jnp.int32)
    start = jnp.int32(0)
    for j in range(4):
        length = lengths[0, j]
        low = jnp.where((rows >= start) & (rows < start + length), start, low)
        start = start + ((length + 127) >> 7) * 128
    return low


def visible_block(low, rb, tb):
    rs = slice(rb * BLOCK, (rb + 1) * BLOCK)
    keys = iota((BLOCK, BLOCK), 0) + tb * BLOCK
    seen = keys >= low[:, rs]
    if tb == rb:
        seen = seen & (keys <= iota((BLOCK, BLOCK), 1) + rb * BLOCK)
    return seen


def masked_head(x, h, scale=None):
    rows = iota(x.shape, 0)
    x = jnp.where((rows >= h * HEAD) & (rows < (h + 1) * HEAD), x, 0.0)
    if scale is not None:
        x = x * scale
    return x.astype(BF)


def shard_loads(c, shards, xn, up, sems):
    loads = []
    for i, rel in enumerate(REL):
        to = at(place_of(c, rel))
        loads.append(pltpu.make_async_copy(shards[i], xn.at[:, to], sems.at[i]))
        loads.append(pltpu.make_async_copy(shards[8 + i], up.at[:, to], sems.at[8 + i]))
    return loads


def forward_kernel(lengths, ctx, wt, w_out, *refs):
    shards, results, (att, sums) = refs[:16], refs[16:19], refs[19:21]
    xn, up, slopes, proj, gh, sems, out_sems = refs[21:]
    loads = shard_loads(ctx[0], shards, xn, up, sems)
    for load in loads:
        load.start()
    for load in loads:
        load.wait()
    for n in range(GROUP // BLOCK):
        cols = slice(n * BLOCK, (n + 1) * BLOCK)
        p = dot(wt[...], xn[:, cols])
        sig = sigmoid(p)
        out = p * sig
        slopes[:, cols] = (sig + out * (1.0 - sig)).astype(BF)
        proj[:, cols] = out.astype(BF)
        gh[:, cols] = dot(w_out[...], up[:, cols])
    stores = [
        pltpu.make_async_copy(v, out, out_sems.at[i])
        for i, (v, out) in enumerate(zip((slopes, proj, gh), results))
    ]
    for store in stores:
        store.start()
    low = first_visible(lengths)
    keys = proj[3 * WIDE :, :].astype(F32).T.astype(BF)
    for rb in range(GROUP // BLOCK):
        rs = slice(rb * BLOCK, (rb + 1) * BLOCK)
        query = proj[2 * WIDE : 3 * WIDE, rs].astype(F32)
        for h in range(2):
            hs = slice(h * HEAD, (h + 1) * HEAD)
            q = masked_head(query, h, 0.125)
            total = jnp.zeros((HEAD, BLOCK), F32)
            for tb in range(rb + 1):
                ts = slice(tb * BLOCK, (tb + 1) * BLOCK)
                s = dot(keys[ts], q)
                w = jnp.where(visible_block(low, rb, tb), s * sigmoid(s), 0.0).astype(BF)
                total = total + dot(proj[WIDE + h * HEAD : WIDE + (h + 1) * HEAD, ts], w)
            att[hs, rs] = total
    a = att[...]
    mean = jnp.mean(a, axis=0, keepdims=True)
    dev = a - mean
    gz = gh[...] * proj[:WIDE, :].astype(F32)
    sums[0:1, :] = mean
    sums[1:2, :] = jnp.sum(dev * dev, axis=0, keepdims=True)
    sums[2:3, :] = jnp.sum(gz, axis=0, keepdims=True)
    sums[3:4, :] = jnp.sum(gz * dev, axis=0, keepdims=True)
    sums[4:8, :] = jnp.zeros((4, GROUP), F32)
    for store in stores:
        store.wait()


def backward_kernel(lengths, ctx, slopes, proj, att, gh, *refs):
    sums, shards = refs[:8], refs[8:24]
    own, other, up_part, down_part, far_up, far_down, weights = refs[24:31]
    gp, gatt, dk, dv, xn, up, sems, out_sems = refs[31:]
    c = ctx[0]
    loads = shard_loads(c, shards, xn, up, sems)
    for load in loads:
        load.start()
    each = [s[...] for s in sums]
    mean = sum(s[0:1, :] for s in each) * (1.0 / N_CTX)
    spread = sum(s[1:2, :] + WIDE * jnp.square(s[0:1, :] - mean) for s in each)
    inverse = lax.rsqrt(spread * (1.0 / D) + EPS)
    first = sum(s[2:3, :] for s in each) * (1.0 / D)
    second = sum(s[3:4, :] + (s[0:1, :] - mean) * s[2:3, :] for s in each) * inverse * (1.0 / D)
    for n in range(GROUP // BLOCK):
        cols = slice(n * BLOCK, (n + 1) * BLOCK)
        z = (att[:, cols] - mean[:, cols]) * inverse[:, cols]
        gate = proj[:WIDE, cols].astype(F32)
        grad = gh[:, cols]
        gp[:WIDE, cols] = (z * gate).astype(BF)
        gp[WIDE : 2 * WIDE, cols] = (grad * z * slopes[:WIDE, cols].astype(F32)).astype(BF)
        rest = grad * gate - first[:, cols] - z * second[:, cols]
        gatt[:, cols] = (inverse[:, cols] * rest).astype(BF)

    low = first_visible(lengths)
    keys = proj[3 * WIDE :, :].astype(F32).T.astype(BF)
    values = proj[WIDE : 2 * WIDE, :].astype(F32).T.astype(BF)
    dk[...] = jnp.zeros((WIDE, GROUP), F32)
    dv[...] = jnp.zeros((WIDE, GROUP), F32)
    for rb in range(GROUP // BLOCK):
        rs = slice(rb * BLOCK, (rb + 1) * BLOCK)
        query = proj[2 * WIDE : 3 * WIDE, rs].astype(F32)
        grad = gatt[:, rs].astype(F32)
        for h in range(2):
            hs = slice(h * HEAD, (h + 1) * HEAD)
            q = masked_head(query, h, 0.125)
            g = masked_head(grad, h)
            total = jnp.zeros((HEAD, BLOCK), F32)
            for tb in range(rb + 1):
                ts = slice(tb * BLOCK, (tb + 1) * BLOCK)
                s = dot(keys[ts], q)
                gw = dot(values[ts], g)
                seen = visible_block(low, rb, tb)
                sig = sigmoid(s)
                w = jnp.where(seen, s * sig, 0.0)
                gs = jnp.where(seen, gw * (sig + w * (1.0 - sig)), 0.0).astype(BF)
                dv[hs, ts] += dot(g[hs], w.astype(BF), NT)
                dk[hs, ts] += dot(q[hs], gs, NT)
                total = total + dot(proj[3 * WIDE + h * HEAD : 3 * WIDE + (h + 1) * HEAD, ts], gs)
            qs = slice(2 * WIDE + h * HEAD, 2 * WIDE + (h + 1) * HEAD)
            to = slice(3 * WIDE + h * HEAD, 3 * WIDE + (h + 1) * HEAD)
            gp[to, rs] = (total * 0.125 * slopes[qs, rs].astype(F32)).astype(BF)
    gp[2 * WIDE : 3 * WIDE, :] = (dv[...] * slopes[WIDE : 2 * WIDE, :].astype(F32)).astype(BF)
    gp[4 * WIDE :, :] = (dk[...] * slopes[3 * WIDE :, :].astype(F32)).astype(BF)

    n, half = PART, PART // 2
    moves = []
    for core in range(2):
        opposite = gp.at[:, at(place_of(c, (2, core)))]
        mine = pl.ds(core * half, half)
        moves += [
            (gp.at[:, at(place_of(c, (0, core)))], (own, other)[core]),
            (gp.at[:, at(place_of(c, (1, core)))], up_part.at[pl.ds(core * n, n), :]),
            (gp.at[:, at(place_of(c, (3, core)))], down_part.at[pl.ds(core * n, n), :]),
            (opposite.at[pl.ds(0, half), :], far_up.at[mine, :]),
            (opposite.at[pl.ds(half, half), :], far_down.at[mine, :]),
        ]
    stores = [pltpu.make_async_copy(*m, out_sems.at[i]) for i, m in enumerate(moves)]
    for store in stores:
        store.start()

    for load in loads:
        load.wait()
    for n in range(4):
        rows = slice(n * BLOCK, (n + 1) * BLOCK)
        part = dot(xn[rows, :], gp[WIDE:, :], NT).astype(BF)
        weights[4 * n : 4 * n + 4, :64, :] = part.reshape(4, 64, 4 * WIDE)
    mix = [dot(gp[:WIDE, :], up[h : h + 512, :], NT).reshape(N_DP, 8, 512) for h in (0, 512)]
    weights[:, 64:, :] = jnp.concatenate(mix, axis=1).astype(BF)
    for store in stores:
        store.wait()


def sum_kernel(ctx, recv, *refs):
    own, other, chips, mixing, total = refs[0], refs[1], refs[2:5], refs[5], refs[6]
    got = recv[0].astype(F32)
    for d in range(1, N_DP):
        got = got + recv[d].astype(F32)
    total[...] = got[:64]
    mixing[:, :512] = got[64:72]
    mixing[:, 512:] = got[72:]

    def rows(rel):
        return total[pl.ds(pl.multiple_of(place_of(ctx[0], rel) * 8, 8), 8), :]

    own[...] = rows((0, 0))
    other[...] = rows((0, 1))
    for step, part in zip((1, 2, 3), chips):
        part[:8, :] = rows((step, 0))
        part[8:, :] = rows((step, 1))


def join_kernel(ctx, mixing, *refs):
    parts, out, mixing_out = refs[:8], refs[8], refs[9]
    mixing_out[...] = mixing[...]
    for i, part in enumerate(parts):
        core = i % 2
        src = place_of(ctx[0], ((4 - i // 2) % 4, core))
        got = part[...] if i < 2 else part[core * 8 : core * 8 + 8, :]
        for kind in range(4):
            out[:, at(kind * 8 + src)] = got[:, kind * WIDE : (kind + 1) * WIDE]


def rows_kernel(ctx, place, w, w_out, *refs):
    parts, out, (hid, gp) = refs[:10], refs[10], refs[11:]
    back = (place[...] == iota((R, R), 0)).astype(BF)

    @pl.when(pl.program_id(0) == 0)
    def _():
        c = ctx[0]
        n, half = PART, PART // 2
        hidden = [None] * 8
        for core in range(2):
            near = slice(core * n, core * n + n)
            rest = slice(core * half, core * half + half)
            far = [parts[6 + core][rest, :], parts[8 + core][rest, :]]
            got = [
                ((0, core), parts[core][...]),
                ((3, core), parts[2 + core][near, :]),
                ((1, core), parts[4 + core][near, :]),
                ((2, core), jnp.concatenate(far, axis=0)),
            ]
            for rel, part in got:
                src = place_of(c, rel)
                hid[:, at(src)] = dot(back, part[:WIDE, :], NT).astype(BF)
                for kind in range(4):
                    start = (kind + 1) * WIDE
                    gp[at(kind * 8 + src), :] = part[start : start + WIDE, :]

    o = dot(hid[...], w_out[...])
    gx = dot(back, dot(w[...], gp[...]).astype(BF), NT)
    cols = gx.shape[1]
    values = [v.reshape(N_DP, 8, cols) for v in (o, gx)]
    out[...] = jnp.concatenate(values, axis=1).reshape(2 * R, cols).astype(BF)


def unpack_kernel(recv, hist, gout, order, out, grad):
    got = recv[...].astype(F32).reshape(N_DP, 2, 8, D)
    back = (order[...] == iota((R, R), 0)).astype(BF)
    o = dot(back, got[:, 0].reshape(R, D).astype(BF))
    gx = dot(back, got[:, 1].reshape(R, D).astype(BF))
    x = hist[...].astype(F32)
    out[...] = (o + x).astype(BF)
    normed, inverse = row_norm(x)
    first = jnp.mean(gx, axis=-1, keepdims=True)
    second = jnp.mean(gx * normed, axis=-1, keepdims=True)
    grad[...] = (inverse * (gx - first - normed * second) + gout[...].astype(F32)).astype(BF)


def own_weights(ctx_s, w_project):
    return pl.pallas_call(
        own_weights_kernel,
        grid_spec=pltpu.PrefetchScalarGridSpec(
            num_scalar_prefetch=1,
            grid=(4,),
            in_specs=[pl.BlockSpec((D, WIDE), lambda k, ctx: (0, k * N_CTX + ctx[0]))],
            out_specs=pl.BlockSpec((WIDE, D), lambda k, ctx: (k, 0)),
        ),
        out_shape=pltpu.HBM((4 * WIDE, D), BF),
        compiler_params=pltpu.CompilerParams(vmem_limit_bytes=VMEM_BYTES),
    )(ctx_s, w_project)


def own_rows(ctx_s, w_out):
    return pl.pallas_call(
        copy_kernel,
        grid_spec=pltpu.PrefetchScalarGridSpec(
            num_scalar_prefetch=1,
            grid=(1,),
            in_specs=[pl.BlockSpec((WIDE, D), lambda k, ctx: (ctx[0], 0))],
            out_specs=pl.BlockSpec((WIDE, D), lambda k, ctx: (0, 0)),
        ),
        out_shape=pltpu.HBM((WIDE, D), BF),
        compiler_params=pltpu.CompilerParams(vmem_limit_bytes=VMEM_BYTES),
    )(ctx_s, w_out)


def rows_back(ctx_s, place, w_project, w_out, parts):
    cols = 512
    whole = pl.BlockSpec(memory_space=pltpu.VMEM)
    return pl.pallas_call(
        rows_kernel,
        grid=(D // cols,),
        in_specs=[
            pl.BlockSpec(memory_space=pltpu.SMEM),
            whole,
            pl.BlockSpec((cols, 4 * D), lambda n: (n, 0)),
            pl.BlockSpec((D, cols), lambda n: (0, n)),
        ]
        + [whole] * 10,
        out_specs=pl.BlockSpec((2 * R, cols), lambda n: (0, n)),
        out_shape=pltpu.HBM((2 * R, D), BF),
        scratch_shapes=[pltpu.VMEM((R, D), BF), pltpu.VMEM((4 * D, R), BF)],
        compiler_params=pltpu.CompilerParams(vmem_limit_bytes=VMEM_BYTES),
    )(ctx_s, place, w_project, w_out, *parts)


def across(x, axis):
    return lax.all_to_all(x, axis, split_axis=0, concat_axis=0, tiled=True)


def local(history, grad_output, lengths, send_order, place_order, w_project, w_out):
    ctx_s = lax.axis_index("ctx").astype(jnp.int32).reshape(1)
    w_project, w_out = hbm(w_project), hbm(w_out)
    order = hbm(send_order.reshape(1, R))
    place = place_order.reshape(1, R)

    (packed,) = call(pack_kernel, [((2 * R, D), BF)], hbm(history), hbm(grad_output), order)
    w_own, w_out_own = own_weights(ctx_s, w_project), own_rows(ctx_s, w_out)
    arrived = across(packed, "dp")
    shard = call(place_kernel, [((D, R), BF)] * 2, arrived, place, late=(w_own, w_out_own))
    shards = [hbm(v) for v in ring_gather(*shard)]
    slopes, proj, gh, att, sums = call(
        forward_kernel,
        [
            ((4 * WIDE, GROUP), BF),
            ((4 * WIDE, GROUP), BF),
            ((WIDE, GROUP), F32),
            ((WIDE, GROUP), F32),
            ((8, GROUP), F32),
        ],
        lengths,
        ctx_s,
        w_own,
        w_out_own,
        *shards,
        smem=2,
        plain=16,
        plain_outs=3,
        scratch=[
            pltpu.VMEM((D, GROUP), BF),
            pltpu.VMEM((D, GROUP), BF),
            pltpu.VMEM((4 * WIDE, GROUP), BF),
            pltpu.VMEM((4 * WIDE, GROUP), BF),
            pltpu.VMEM((WIDE, GROUP), F32),
            pltpu.SemaphoreType.DMA((16,)),
            pltpu.SemaphoreType.DMA((3,)),
        ],
    )
    all_sums = [sums] + [send(sums, step, 0) for step in (2, 1, 3)]
    all_sums += [send(v, 0, 1) for v in all_sums]
    own, other, up_part, down_part, far_up, far_down, weights = call(
        backward_kernel,
        [
            ((PART, R), BF),
            ((PART, R), BF),
            ((2 * PART, R), BF),
            ((2 * PART, R), BF),
            ((PART, R), BF),
            ((PART, R), BF),
            ((N_DP, 80, 4 * WIDE), BF),
        ],
        lengths,
        ctx_s,
        *[hbm(v) for v in (slopes, proj, att, gh)],
        *all_sums,
        *shards,
        smem=2,
        plain=16,
        plain_outs=6,
        scratch=[
            pltpu.VMEM((PART, GROUP), BF),
            pltpu.VMEM((WIDE, GROUP), BF),
            pltpu.VMEM((WIDE, GROUP), F32),
            pltpu.VMEM((WIDE, GROUP), F32),
            pltpu.VMEM((D, GROUP), BF),
            pltpu.VMEM((D, GROUP), BF),
            pltpu.SemaphoreType.DMA((16,)),
            pltpu.SemaphoreType.DMA((10,)),
        ],
    )
    parts = relay(own, other, (up_part, down_part), (far_up, far_down))
    weights = across(weights, "dp")
    rows = rows_back(ctx_s, place, w_project, w_out, parts)
    own, other, *chips, mixing = call(
        sum_kernel,
        [((8, 4 * WIDE), F32)] * 2 + [((16, 4 * WIDE), F32)] * 3 + [((8, D), F32)],
        ctx_s,
        weights,
        smem=1,
        late=(rows,),
        scratch=[pltpu.VMEM((64, 4 * WIDE), F32)],
    )
    owners = [(d * 8 + c, (2 * c + d // 8) * 8 + d % 8) for d in range(N_DP) for c in range(N_CTX)]
    mixing = lax.ppermute(mixing, ("dp", "ctx"), owners)
    project = [own, send(other, 0, 1)]
    for step, part in zip((1, 2, 3), chips):
        part = send(part, step, 0)
        project += [part, send(part, 0, 1)]
    returned = across(rows, "dp")
    output, input_grad = call(
        unpack_kernel, [((R, D), BF), ((R, D), BF)], returned, history, grad_output, order
    )
    project_grad, mixing_grad = call(
        join_kernel, [((8, 4 * D), F32), ((8, D), F32)], ctx_s, mixing, *project, smem=1
    )
    return output, input_grad, project_grad, mixing_grad


def solution(mesh):
    rows = P(("dp", "ctx"), None)
    ids = P(("dp", "ctx"))
    return jax.shard_map(
        local,
        mesh=mesh,
        in_specs=(rows, rows, P("dp", None), ids, ids, P(), P()),
        out_specs=(rows, rows, rows, rows),
        check_vma=False,
    )
```

```python
import jax
import jax.numpy as jnp
from jax import lax
from jax.experimental import pallas as pl
from jax.experimental.pallas import tpu as pltpu
from jax.sharding import PartitionSpec as P


D = 1024
WIDE = 128
PART = 5 * WIDE
HEAD = 64
N_DP = 16
N_CTX = 8
R = 128
GROUP = 1024
BLOCK = 256
EPS = 1e-6
BF = jnp.bfloat16
F32 = jnp.float32
NN = (((1,), (0,)), ((), ()))
NT = (((1,), (1,)), ((), ()))
VMEM_BYTES = 32 * 1024 * 1024


def dot(a, b, dims=NN):
    return lax.dot_general(a, b, dims, preferred_element_type=F32)


def sigmoid(v):
    return 0.5 * jnp.tanh(0.5 * v) + 0.5


def iota(shape, dim):
    return lax.broadcasted_iota(jnp.int32, shape, dim)


def row_norm(values):
    centred = values - jnp.mean(values, axis=-1, keepdims=True)
    inverse = lax.rsqrt(jnp.mean(centred * centred, axis=-1, keepdims=True) + EPS)
    return centred * inverse, inverse


def skip(body, first, count):
    def kernel(*refs):
        body(*refs[:first], *refs[first + count :])

    return kernel if count else body


def hbm(x):
    return pltpu.with_memory_space_constraint(x, pltpu.HBM)


def call(body, outs, *args, smem=0, plain=0, plain_outs=0, scratch=(), late=()):
    specs = [pl.BlockSpec(memory_space=pltpu.SMEM)] * smem
    specs += [pl.BlockSpec(memory_space=pltpu.VMEM)] * (len(args) - smem - plain)
    specs += [pl.BlockSpec(memory_space=pl.ANY)] * (plain + len(late))
    return pl.pallas_call(
        skip(body, len(args), len(late)),
        out_shape=[pltpu.HBM(s, t) for s, t in outs],
        in_specs=specs,
        out_specs=[pl.BlockSpec(memory_space=pl.ANY)] * plain_outs
        + [pl.BlockSpec(memory_space=pltpu.VMEM)] * (len(outs) - plain_outs),
        scratch_shapes=list(scratch),
        compiler_params=pltpu.CompilerParams(vmem_limit_bytes=VMEM_BYTES),
    )(*args, *late)


REL = [(0, 0), (0, 1), (1, 0), (1, 1), (2, 0), (2, 1), (3, 0), (3, 1)]


def place_of(ctx, rel):
    chip = lax.rem((ctx >> 1) + rel[0], 4)
    return chip * 2 + ((ctx & 1) ^ rel[1])


def send(x, step, flip):
    pairs = [(2 * a + b, 2 * ((a + step) % 4) + (b ^ flip)) for a in range(4) for b in range(2)]
    return lax.ppermute(x, "ctx", pairs)


def ring_gather(a, b):
    a_up, b_down = send(a, 3, 0), send(b, 1, 0)
    a_far, b_far = send(a_up, 3, 0), send(b_down, 1, 0)
    b_up, a_down = send(b, 3, 0), send(a, 1, 0)
    got = []
    for v in (a, a_up, a_far, a_down, b, b_up, b_far, b_down):
        got += [v, send(v, 0, 1)]
    return got


def relay(own, other, near, far):
    far = [send(send(far[0], 1, 0), 1, 0), send(send(far[1], 3, 0), 3, 0)]
    near = [send(near[0], 1, 0), send(near[1], 3, 0)]
    got = [own, send(other, 0, 1)]
    for v in near + far:
        got += [v, send(v, 0, 1)]
    return got


def at(index):
    return pl.ds(pl.multiple_of(index * R, R), R)


def copy_kernel(ctx, x, out):
    del ctx
    out[...] = x[...]


def pick_rows(ids):
    return (ids == iota((R, R), 0)).astype(F32).T.astype(BF)


def pack_kernel(hist, gout, order, out):
    xn = row_norm(hist[...].astype(F32))[0].astype(BF)
    pick = pick_rows(order[...])
    a = dot(pick, xn).reshape(N_DP, 8, D)
    b = dot(pick, gout[...]).reshape(N_DP, 8, D)
    out[...] = jnp.concatenate([a, b], axis=1).reshape(2 * R, D).astype(BF)


def own_weights_kernel(ctx, w, out):
    del ctx
    out[...] = w[...].astype(F32).T.astype(BF)


def place_kernel(recv, place, *outs):
    pick = pick_rows(place[...])
    got = recv[...].astype(F32).reshape(N_DP, 2, 8, D)
    for i in range(2):
        rows = dot(pick, got[:, i].reshape(R, D).astype(BF))
        outs[i][...] = rows.T.astype(BF)


def first_visible(lengths):
    rows = iota((1, GROUP), 1)
    low = jnp.full((1, GROUP), 1 << 20, jnp.int32)
    start = jnp.int32(0)
    for j in range(4):
        length = lengths[0, j]
        low = jnp.where((rows >= start) & (rows < start + length), start, low)
        start = start + ((length + 127) >> 7) * 128
    return low


def visible_block(low, rb, tb):
    rs = slice(rb * BLOCK, (rb + 1) * BLOCK)
    keys = iota((BLOCK, BLOCK), 0) + tb * BLOCK
    seen = keys >= low[:, rs]
    if tb == rb:
        seen = seen & (keys <= iota((BLOCK, BLOCK), 1) + rb * BLOCK)
    return seen


def masked_head(x, h, scale=None):
    rows = iota(x.shape, 0)
    x = jnp.where((rows >= h * HEAD) & (rows < (h + 1) * HEAD), x, 0.0)
    if scale is not None:
        x = x * scale
    return x.astype(BF)


def shard_loads(c, shards, xn, up, sems):
    loads = []
    for i, rel in enumerate(REL):
        to = at(place_of(c, rel))
        loads.append(pltpu.make_async_copy(shards[i], xn.at[:, to], sems.at[i]))
        loads.append(pltpu.make_async_copy(shards[8 + i], up.at[:, to], sems.at[8 + i]))
    return loads


def forward_kernel(lengths, ctx, wt, w_out, *refs):
    shards, results, (att, sums) = refs[:16], refs[16:19], refs[19:21]
    xn, up, slopes, proj, gh, sems, out_sems = refs[21:]
    loads = shard_loads(ctx[0], shards, xn, up, sems)
    for load in loads:
        load.start()
    for load in loads:
        load.wait()
    for n in range(GROUP // BLOCK):
        cols = slice(n * BLOCK, (n + 1) * BLOCK)
        p = dot(wt[...], xn[:, cols])
        sig = sigmoid(p)
        out = p * sig
        slopes[:, cols] = (sig + out * (1.0 - sig)).astype(BF)
        proj[:, cols] = out.astype(BF)
        gh[:, cols] = dot(w_out[...], up[:, cols])
    stores = [
        pltpu.make_async_copy(v, out, out_sems.at[i])
        for i, (v, out) in enumerate(zip((slopes, proj, gh), results))
    ]
    for store in stores:
        store.start()
    low = first_visible(lengths)
    keys = proj[3 * WIDE :, :].astype(F32).T.astype(BF)
    for rb in range(GROUP // BLOCK):
        rs = slice(rb * BLOCK, (rb + 1) * BLOCK)
        query = proj[2 * WIDE : 3 * WIDE, rs].astype(F32)
        for h in range(2):
            hs = slice(h * HEAD, (h + 1) * HEAD)
            q = masked_head(query, h, 0.125)
            total = jnp.zeros((HEAD, BLOCK), F32)
            for tb in range(rb + 1):
                ts = slice(tb * BLOCK, (tb + 1) * BLOCK)
                s = dot(keys[ts], q)
                w = jnp.where(visible_block(low, rb, tb), s * sigmoid(s), 0.0).astype(BF)
                total = total + dot(proj[WIDE + h * HEAD : WIDE + (h + 1) * HEAD, ts], w)
            att[hs, rs] = total
    a = att[...]
    mean = jnp.mean(a, axis=0, keepdims=True)
    dev = a - mean
    gz = gh[...] * proj[:WIDE, :].astype(F32)
    sums[0:1, :] = mean
    sums[1:2, :] = jnp.sum(dev * dev, axis=0, keepdims=True)
    sums[2:3, :] = jnp.sum(gz, axis=0, keepdims=True)
    sums[3:4, :] = jnp.sum(gz * dev, axis=0, keepdims=True)
    sums[4:8, :] = jnp.zeros((4, GROUP), F32)
    for store in stores:
        store.wait()


def backward_kernel(lengths, ctx, slopes, proj, att, gh, *refs):
    sums, shards = refs[:8], refs[8:24]
    own, other, up_part, down_part, far_up, far_down, weights = refs[24:31]
    gp, gatt, dk, dv, xn, up, sems, out_sems = refs[31:]
    c = ctx[0]
    loads = shard_loads(c, shards, xn, up, sems)
    for load in loads:
        load.start()
    each = [s[...] for s in sums]
    mean = sum(s[0:1, :] for s in each) * (1.0 / N_CTX)
    spread = sum(s[1:2, :] + WIDE * jnp.square(s[0:1, :] - mean) for s in each)
    inverse = lax.rsqrt(spread * (1.0 / D) + EPS)
    first = sum(s[2:3, :] for s in each) * (1.0 / D)
    second = sum(s[3:4, :] + (s[0:1, :] - mean) * s[2:3, :] for s in each) * inverse * (1.0 / D)
    for n in range(GROUP // BLOCK):
        cols = slice(n * BLOCK, (n + 1) * BLOCK)
        z = (att[:, cols] - mean[:, cols]) * inverse[:, cols]
        gate = proj[:WIDE, cols].astype(F32)
        grad = gh[:, cols]
        gp[:WIDE, cols] = (z * gate).astype(BF)
        gp[WIDE : 2 * WIDE, cols] = (grad * z * slopes[:WIDE, cols].astype(F32)).astype(BF)
        rest = grad * gate - first[:, cols] - z * second[:, cols]
        gatt[:, cols] = (inverse[:, cols] * rest).astype(BF)

    low = first_visible(lengths)
    keys = proj[3 * WIDE :, :].astype(F32).T.astype(BF)
    values = proj[WIDE : 2 * WIDE, :].astype(F32).T.astype(BF)
    dk[...] = jnp.zeros((WIDE, GROUP), F32)
    dv[...] = jnp.zeros((WIDE, GROUP), F32)
    for rb in range(GROUP // BLOCK):
        rs = slice(rb * BLOCK, (rb + 1) * BLOCK)
        query = proj[2 * WIDE : 3 * WIDE, rs].astype(F32)
        grad = gatt[:, rs].astype(F32)
        for h in range(2):
            hs = slice(h * HEAD, (h + 1) * HEAD)
            q = masked_head(query, h, 0.125)
            g = masked_head(grad, h)
            total = jnp.zeros((HEAD, BLOCK), F32)
            for tb in range(rb + 1):
                ts = slice(tb * BLOCK, (tb + 1) * BLOCK)
                s = dot(keys[ts], q)
                gw = dot(values[ts], g)
                seen = visible_block(low, rb, tb)
                sig = sigmoid(s)
                w = jnp.where(seen, s * sig, 0.0)
                gs = jnp.where(seen, gw * (sig + w * (1.0 - sig)), 0.0).astype(BF)
                dv[hs, ts] += dot(g[hs], w.astype(BF), NT)
                dk[hs, ts] += dot(q[hs], gs, NT)
                total = total + dot(proj[3 * WIDE + h * HEAD : 3 * WIDE + (h + 1) * HEAD, ts], gs)
            qs = slice(2 * WIDE + h * HEAD, 2 * WIDE + (h + 1) * HEAD)
            to = slice(3 * WIDE + h * HEAD, 3 * WIDE + (h + 1) * HEAD)
            gp[to, rs] = (total * 0.125 * slopes[qs, rs].astype(F32)).astype(BF)
    gp[2 * WIDE : 3 * WIDE, :] = (dv[...] * slopes[WIDE : 2 * WIDE, :].astype(F32)).astype(BF)
    gp[4 * WIDE :, :] = (dk[...] * slopes[3 * WIDE :, :].astype(F32)).astype(BF)

    n, half = PART, PART // 2
    moves = []
    for core in range(2):
        opposite = gp.at[:, at(place_of(c, (2, core)))]
        mine = pl.ds(core * half, half)
        moves += [
            (gp.at[:, at(place_of(c, (0, core)))], (own, other)[core]),
            (gp.at[:, at(place_of(c, (1, core)))], up_part.at[pl.ds(core * n, n), :]),
            (gp.at[:, at(place_of(c, (3, core)))], down_part.at[pl.ds(core * n, n), :]),
            (opposite.at[pl.ds(0, half), :], far_up.at[mine, :]),
            (opposite.at[pl.ds(half, half), :], far_down.at[mine, :]),
        ]
    stores = [pltpu.make_async_copy(*m, out_sems.at[i]) for i, m in enumerate(moves)]
    for store in stores:
        store.start()

    for load in loads:
        load.wait()
    for n in range(4):
        rows = slice(n * BLOCK, (n + 1) * BLOCK)
        part = dot(xn[rows, :], gp[WIDE:, :], NT).astype(BF)
        weights[4 * n : 4 * n + 4, :64, :] = part.reshape(4, 64, 4 * WIDE)
    mix = [dot(gp[:WIDE, :], up[h : h + 512, :], NT).reshape(N_DP, 8, 512) for h in (0, 512)]
    weights[:, 64:, :] = jnp.concatenate(mix, axis=1).astype(BF)
    for store in stores:
        store.wait()


def sum_kernel(ctx, recv, *refs):
    own, other, chips, mixing, total = refs[0], refs[1], refs[2:5], refs[5], refs[6]
    got = recv[0].astype(F32)
    for d in range(1, N_DP):
        got = got + recv[d].astype(F32)
    total[...] = got[:64]
    mixing[:, :512] = got[64:72]
    mixing[:, 512:] = got[72:]

    def rows(rel):
        return total[pl.ds(pl.multiple_of(place_of(ctx[0], rel) * 8, 8), 8), :]

    own[...] = rows((0, 0))
    other[...] = rows((0, 1))
    for step, part in zip((1, 2, 3), chips):
        part[:8, :] = rows((step, 0))
        part[8:, :] = rows((step, 1))


def join_kernel(ctx, mixing, *refs):
    parts, out, mixing_out = refs[:8], refs[8], refs[9]
    mixing_out[...] = mixing[...]
    for i, part in enumerate(parts):
        core = i % 2
        src = place_of(ctx[0], ((4 - i // 2) % 4, core))
        got = part[...] if i < 2 else part[core * 8 : core * 8 + 8, :]
        for kind in range(4):
            out[:, at(kind * 8 + src)] = got[:, kind * WIDE : (kind + 1) * WIDE]


def rows_kernel(ctx, place, w, w_out, *refs):
    parts, out, (hid, gp) = refs[:10], refs[10], refs[11:]
    back = (place[...] == iota((R, R), 0)).astype(BF)

    @pl.when(pl.program_id(0) == 0)
    def _():
        c = ctx[0]
        n, half = PART, PART // 2
        hidden = [None] * 8
        for core in range(2):
            near = slice(core * n, core * n + n)
            rest = slice(core * half, core * half + half)
            far = [parts[6 + core][rest, :], parts[8 + core][rest, :]]
            got = [
                ((0, core), parts[core][...]),
                ((3, core), parts[2 + core][near, :]),
                ((1, core), parts[4 + core][near, :]),
                ((2, core), jnp.concatenate(far, axis=0)),
            ]
            for rel, part in got:
                src = place_of(c, rel)
                hid[:, at(src)] = dot(back, part[:WIDE, :], NT).astype(BF)
                for kind in range(4):
                    start = (kind + 1) * WIDE
                    gp[at(kind * 8 + src), :] = part[start : start + WIDE, :]

    o = dot(hid[...], w_out[...])
    gx = dot(back, dot(w[...], gp[...]).astype(BF), NT)
    cols = gx.shape[1]
    values = [v.reshape(N_DP, 8, cols) for v in (o, gx)]
    out[...] = jnp.concatenate(values, axis=1).reshape(2 * R, cols).astype(BF)


def unpack_kernel(recv, hist, gout, order, out, grad):
    got = recv[...].astype(F32).reshape(N_DP, 2, 8, D)
    back = (order[...] == iota((R, R), 0)).astype(BF)
    o = dot(back, got[:, 0].reshape(R, D).astype(BF))
    gx = dot(back, got[:, 1].reshape(R, D).astype(BF))
    x = hist[...].astype(F32)
    out[...] = (o + x).astype(BF)
    normed, inverse = row_norm(x)
    first = jnp.mean(gx, axis=-1, keepdims=True)
    second = jnp.mean(gx * normed, axis=-1, keepdims=True)
    grad[...] = (inverse * (gx - first - normed * second) + gout[...].astype(F32)).astype(BF)


def own_weights(ctx_s, w_project):
    return pl.pallas_call(
        own_weights_kernel,
        grid_spec=pltpu.PrefetchScalarGridSpec(
            num_scalar_prefetch=1,
            grid=(4,),
            in_specs=[pl.BlockSpec((D, WIDE), lambda k, ctx: (0, k * N_CTX + ctx[0]))],
            out_specs=pl.BlockSpec((WIDE, D), lambda k, ctx: (k, 0)),
        ),
        out_shape=pltpu.HBM((4 * WIDE, D), BF),
        compiler_params=pltpu.CompilerParams(vmem_limit_bytes=VMEM_BYTES),
    )(ctx_s, w_project)


def own_rows(ctx_s, w_out):
    return pl.pallas_call(
        copy_kernel,
        grid_spec=pltpu.PrefetchScalarGridSpec(
            num_scalar_prefetch=1,
            grid=(1,),
            in_specs=[pl.BlockSpec((WIDE, D), lambda k, ctx: (ctx[0], 0))],
            out_specs=pl.BlockSpec((WIDE, D), lambda k, ctx: (0, 0)),
        ),
        out_shape=pltpu.HBM((WIDE, D), BF),
        compiler_params=pltpu.CompilerParams(vmem_limit_bytes=VMEM_BYTES),
    )(ctx_s, w_out)


def rows_back(ctx_s, place, w_project, w_out, parts):
    cols = 512
    whole = pl.BlockSpec(memory_space=pltpu.VMEM)
    return pl.pallas_call(
        rows_kernel,
        grid=(D // cols,),
        in_specs=[
            pl.BlockSpec(memory_space=pltpu.SMEM),
            whole,
            pl.BlockSpec((cols, 4 * D), lambda n: (n, 0)),
            pl.BlockSpec((D, cols), lambda n: (0, n)),
        ]
        + [whole] * 10,
        out_specs=pl.BlockSpec((2 * R, cols), lambda n: (0, n)),
        out_shape=pltpu.HBM((2 * R, D), BF),
        scratch_shapes=[pltpu.VMEM((R, D), BF), pltpu.VMEM((4 * D, R), BF)],
        compiler_params=pltpu.CompilerParams(vmem_limit_bytes=VMEM_BYTES),
    )(ctx_s, place, w_project, w_out, *parts)


def across(x, axis):
    return lax.all_to_all(x, axis, split_axis=0, concat_axis=0, tiled=True)


def local(history, grad_output, lengths, send_order, place_order, w_project, w_out):
    ctx_s = lax.axis_index("ctx").astype(jnp.int32).reshape(1)
    w_project, w_out = hbm(w_project), hbm(w_out)
    order = hbm(send_order.reshape(1, R))
    place = place_order.reshape(1, R)

    (packed,) = call(pack_kernel, [((2 * R, D), BF)], hbm(history), hbm(grad_output), order)
    w_own, w_out_own = own_weights(ctx_s, w_project), own_rows(ctx_s, w_out)
    arrived = across(packed, "dp")
    shard = call(place_kernel, [((D, R), BF)] * 2, arrived, place, late=(w_own, w_out_own))
    shards = [hbm(v) for v in ring_gather(*shard)]
    slopes, proj, gh, att, sums = call(
        forward_kernel,
        [
            ((4 * WIDE, GROUP), BF),
            ((4 * WIDE, GROUP), BF),
            ((WIDE, GROUP), F32),
            ((WIDE, GROUP), F32),
            ((8, GROUP), F32),
        ],
        lengths,
        ctx_s,
        w_own,
        w_out_own,
        *shards,
        smem=2,
        plain=16,
        plain_outs=3,
        scratch=[
            pltpu.VMEM((D, GROUP), BF),
            pltpu.VMEM((D, GROUP), BF),
            pltpu.VMEM((4 * WIDE, GROUP), BF),
            pltpu.VMEM((4 * WIDE, GROUP), BF),
            pltpu.VMEM((WIDE, GROUP), F32),
            pltpu.SemaphoreType.DMA((16,)),
            pltpu.SemaphoreType.DMA((3,)),
        ],
    )
    all_sums = [sums] + [send(sums, step, 0) for step in (2, 1, 3)]
    all_sums += [send(v, 0, 1) for v in all_sums]
    own, other, up_part, down_part, far_up, far_down, weights = call(
        backward_kernel,
        [
            ((PART, R), BF),
            ((PART, R), BF),
            ((2 * PART, R), BF),
            ((2 * PART, R), BF),
            ((PART, R), BF),
            ((PART, R), BF),
            ((N_DP, 80, 4 * WIDE), BF),
        ],
        lengths,
        ctx_s,
        *[hbm(v) for v in (slopes, proj, att, gh)],
        *all_sums,
        *shards,
        smem=2,
        plain=16,
        plain_outs=6,
        scratch=[
            pltpu.VMEM((PART, GROUP), BF),
            pltpu.VMEM((WIDE, GROUP), BF),
            pltpu.VMEM((WIDE, GROUP), F32),
            pltpu.VMEM((WIDE, GROUP), F32),
            pltpu.VMEM((D, GROUP), BF),
            pltpu.VMEM((D, GROUP), BF),
            pltpu.SemaphoreType.DMA((16,)),
            pltpu.SemaphoreType.DMA((10,)),
        ],
    )
    parts = relay(own, other, (up_part, down_part), (far_up, far_down))
    weights = across(weights, "dp")
    rows = rows_back(ctx_s, place, w_project, w_out, parts)
    own, other, *chips, mixing = call(
        sum_kernel,
        [((8, 4 * WIDE), F32)] * 2 + [((16, 4 * WIDE), F32)] * 3 + [((8, D), F32)],
        ctx_s,
        weights,
        smem=1,
        late=(rows,),
        scratch=[pltpu.VMEM((64, 4 * WIDE), F32)],
    )
    owners = [(d * 8 + c, (2 * c + d // 8) * 8 + d % 8) for d in range(N_DP) for c in range(N_CTX)]
    mixing = lax.ppermute(mixing, ("dp", "ctx"), owners)
    project = [own, send(other, 0, 1)]
    for step, part in zip((1, 2, 3), chips):
        part = send(part, step, 0)
        project += [part, send(part, 0, 1)]
    returned = across(rows, "dp")
    output, input_grad = call(
        unpack_kernel, [((R, D), BF), ((R, D), BF)], returned, history, grad_output, order
    )
    project_grad, mixing_grad = call(
        join_kernel, [((8, 4 * D), F32), ((8, D), F32)], ctx_s, mixing, *project, smem=1
    )
    return output, input_grad, project_grad, mixing_grad


def solution(mesh):
    rows = P(("dp", "ctx"), None)
    ids = P(("dp", "ctx"))
    return jax.shard_map(
        local,
        mesh=mesh,
        in_specs=(rows, rows, P("dp", None), ids, ids, P(), P()),
        out_specs=(rows, rows, rows, rows),
        check_vma=False,
    )
```
